512 devices in a mesh: gx: 16 (over z), gy: 8 (over x, core), band: 4 (over y).
Axes of the slice: x: 4, y: 4, z: 16, core: 2. Of those that a mesh axis runs over, the one named last changes fastest.
Arguments:
- orbitals: float32 [32, 128, 64, 128], P('band', 'gx', 'gy'), may hold values from -21 to 21
- delta_potential: float32 [128, 64, 128], P('gx', 'gy'), may hold values from 0.5 to 2
- potential: float32 [128, 64, 128], P('gx', 'gy'), may hold values from -3 to 0
- energies: float32 [4000], replicated, may hold values from -2 to 2
- band_index: int32 [32], P('band'), may hold values from 0 to 3999
Outputs:
- delta_orbitals: float32 [32, 128, 64, 128], P('band', 'gx', 'gy')
- residual: float32 [32, 128, 64, 128], P('band', 'gx', 'gy')
- density: float32 [128, 64, 128], P('gx', 'gy', 'band')
The draws below stay inside these ranges and needn't reach their ends.
All inputs are finite; a program needn't handle non-finite values.
Results may differ from the reference program's by a relative error of at most 0.00028.
Values sent between devices are 32-bit elements; how exact they have to be, the bound alone decides.
A program may use at most 64 MiB of HBM per device.

```python
import math
import jax
import jax.numpy as jnp
from jax import lax

NZ = 128
NE = 4000
ITERS = 2
NB = 32
NX = 128
NY = 64


def draw_orbitals(key, part):
    key = jax.random.fold_in(key, 11)
    scale_key, noise_key = jax.random.split(key)
    scales = jnp.exp(jax.random.uniform(scale_key, (NB, 1, 1, 1), jnp.float32, math.log(0.5), math.log(2.0)))
    along_x = (jnp.arange(NX, dtype=jnp.float32) / NX - 0.5)[None, :, None, None]
    along_y = (jnp.arange(NY, dtype=jnp.float32) / NY - 0.5)[None, None, :, None]
    envelope = jnp.exp(0.5 * math.log(3.0) * (along_x + along_y))
    noise = jnp.clip(jax.random.normal(noise_key, (NB, NX, NY, NZ), jnp.float32), -6.0, 6.0)
    return (scales * envelope * noise).astype(jnp.float32)


def plant(result, stream_key, least, largest):
    longest = result.shape.index(max(result.shape))
    spots = []
    for shift in (0, 1):
        where = [jax.random.randint(jax.random.fold_in(stream_key, axis), (), 0, length) for axis, length in enumerate(result.shape)]
        where[longest] = (where[longest] + shift) % result.shape[longest]
        spots.append(tuple(where))
    return result.at[spots[0]].set(least).at[spots[1]].set(largest)


def block_scale(key, dims, cuts, low, top_value):
    gain = 1.0
    for position, shards_of in cuts:
        draws = jax.random.uniform(jax.random.fold_in(jax.random.fold_in(key, 6), position), (shards_of,), jnp.float32, low / len(cuts), top_value / len(cuts))
        gain = gain * jnp.repeat(jnp.exp(draws), dims[position] // shards_of).reshape((-1,) + (1,) * (len(dims) - 1 - position))
    return gain


def setup_inputs(seed: int = 0) -> dict:
    streams_of = jax.random.split(jax.random.key(seed), 6)
    orbitals = draw_orbitals(jax.random.fold_in(streams_of[5], 71), 0)
    delta_potential = jnp.clip(0.5 + 1.5 * jax.random.uniform(streams_of[1], (NX, NY, NZ), jnp.float32) ** block_scale(streams_of[1], (NX, NY, NZ), ((0, 16), (1, 8)), -0.2, 0.2), 0.5, 2.0)
    potential = jnp.clip(-3.0 + 3.0 * jax.random.uniform(streams_of[2], (NX, NY, NZ), jnp.float32) ** block_scale(streams_of[2], (NX, NY, NZ), ((0, 16), (1, 8)), -0.2, 0.2), -3.0, 0.0)
    energies = jnp.clip(jax.random.uniform(streams_of[3], (NE,), jnp.float32, -2.0, 2.0), -2.0, 2.0)
    band_index = plant(jax.random.randint(streams_of[4], (NB,), 0, NE), jax.random.fold_in(streams_of[4], 1), 0, NE - 1).astype(jnp.int32)
    return dict(orbitals=orbitals, delta_potential=delta_potential, potential=potential, energies=energies, band_index=band_index)


stencil_weights = (-5369.0 / 1800.0, 12.0 / 7.0, -15.0 / 56.0, 10.0 / 189.0, -1.0 / 112.0, 2.0 / 1925.0, -1.0 / 16632.0)
spacing = 0.6
level_shift = 4.0
epsilon = 1e-6
highest = lax.Precision.HIGHEST


def kinetic(values):
    size_x = values.shape[0]
    size_y = values.shape[1]
    padded = jnp.pad(values, ((6, 6), (6, 6), (0, 0)))
    laplace = 3.0 * stencil_weights[0] * values
    for offset in range(1, 7):
        neighbours = padded[6 + offset:6 + offset + size_x, 6:6 + size_y] + padded[6 - offset:6 - offset + size_x, 6:6 + size_y]
        neighbours = neighbours + padded[6:6 + size_x, 6 + offset:6 + offset + size_y] + padded[6:6 + size_x, 6 - offset:6 - offset + size_y]
        neighbours = neighbours + jnp.roll(values, offset, 2) + jnp.roll(values, -offset, 2)
        laplace = laplace + stencil_weights[offset] * neighbours
    return (-0.5 / (spacing * spacing)) * laplace


def intersection(orbitals, vectors):
    return jnp.einsum("mxyz,nxyz->mn", orbitals, vectors, precision=highest) / float(NX * NY * NZ)


def combine(orbitals, coefficients):
    return jnp.einsum("mn,mxyz->nxyz", coefficients, orbitals, precision=highest)


def apply_operator(vectors, orbitals, potential, levels):
    local_part = lax.map(kinetic, vectors) + (potential[None] - levels[:, None, None, None]) * vectors
    return local_part + level_shift * combine(orbitals, intersection(orbitals, vectors))


def reference(orbitals, delta_potential, potential, energies, band_index):
    levels = energies[band_index]
    perturbed = delta_potential[None] * orbitals
    right_side = -(perturbed - combine(orbitals, intersection(orbitals, perturbed)))
    residual = right_side
    delta_orbitals = jnp.zeros_like(orbitals)
    cell_count = float(NX * NY * NZ)
    for iteration in range(ITERS):
        applied = apply_operator(residual, orbitals, potential, levels)
        numerator = jnp.sum(applied * residual, axis=(1, 2, 3)) / cell_count
        denominator = jnp.sum(applied * applied, axis=(1, 2, 3)) / cell_count
        step_length = (numerator / (denominator + epsilon))[:, None, None, None]
        delta_orbitals = delta_orbitals + step_length * residual
        residual = residual - step_length * applied
    density = (4.0 / NB) * jnp.sum(orbitals * delta_orbitals, axis=0)
    return delta_orbitals, residual, density
```

```python
import functools

import jax
import jax.numpy as jnp
from jax import lax
from jax.experimental import pallas as pl
from jax.experimental.pallas import tpu as pltpu
from jax.sharding import PartitionSpec as P

stencil_weights = (
    -5369.0 / 1800.0,
    12.0 / 7.0,
    -15.0 / 56.0,
    10.0 / 189.0,
    -1.0 / 112.0,
    2.0 / 1925.0,
    -1.0 / 16632.0,
)
spacing = 0.6
level_shift = 4.0
epsilon = 1e-06
highest = lax.Precision.HIGHEST
scale = -0.5 / (spacing * spacing)
taps = tuple(scale * w for w in stencil_weights)
MESH = pl.DeviceIdType.MESH
WIDTH = 6


def iota(shape, dim):
    return lax.broadcasted_iota(jnp.int32, shape, dim)


def dot(a, b):
    return jnp.dot(a, b, precision=highest, preferred_element_type=jnp.float32)


def dot_nt(a, b):
    return lax.dot_general(
        a, b, (((1,), (1,)), ((), ())), precision=highest, preferred_element_type=jnp.float32
    )


def rowsum(x):
    return jnp.sum(x, axis=1, keepdims=True)


def lanes(parts):
    return jnp.concatenate(parts, axis=1)


def rows(parts):
    return jnp.concatenate(parts, axis=0)


def kernel(
    sizes,
    o_ref,
    dv_ref,
    v_ref,
    energies_ref,
    index_ref,
    delta_ref,
    residual_ref,
    density_ref,
    o_far,
    ho_own,
    ho_far,
    x_halo,
    y_halo,
    dvx_halo,
    dvy_halo,
    b_own,
    bx_halo,
    by_halo,
    hp_keep,
    src_g,
    src_z,
    slots_g,
    slots_z,
    gram_src_g,
    gram_src_z,
    gram_slots_g,
    gram_slots_z,
    dens_src,
    dens_slots,
    gather_sems,
    halo_sems,
    sum_sems,
    gram_sems,
    dens_sems,
):
    n_gx, n_gy, n_band = sizes
    me = {a: lax.axis_index(a) for a in ("gx", "gy", "band")}
    count = {"gx": n_gx, "gy": n_gy, "band": n_band}
    cells = float(n_gx * n_gy * 8 * 8 * 128)

    def peer(axis, offset):
        return {axis: lax.rem(me[axis] + offset, count[axis])}

    barrier = pltpu.get_barrier_semaphore()
    partners = 0
    for axis in ("band", "gx", "gy"):
        for offset in range(1, count[axis]):
            pl.semaphore_signal(barrier, inc=1, device_id=peer(axis, offset), device_id_type=MESH)
            partners += 1
    pl.semaphore_wait(barrier, partners)

    def send(src, dst, sems, k, axis, offset):
        copy = pltpu.make_async_remote_copy(
            src_ref=src,
            dst_ref=dst,
            send_sem=sems.at[0, k],
            recv_sem=sems.at[1, k],
            device_id=peer(axis, offset),
            device_id_type=MESH,
        )
        copy.start()
        return copy

    def gather_band(own, far, base):
        order = [2, 1, 3] if n_band == 4 else list(range(1, n_band))
        return [send(own, far.at[d - 1], gather_sems, base + d - 1, "band", d) for d in order]

    def halo(field, xh, yh, base):
        return [
            send(field.at[:, 8 - WIDTH : 8], xh.at[0], halo_sems, base, "gx", 1),
            send(field.at[:, 0:WIDTH], xh.at[1], halo_sems, base + 1, "gx", n_gx - 1),
            send(field, yh.at[0], halo_sems, base + 2, "gy", 1),
            send(field, yh.at[1], halo_sems, base + 3, "gy", n_gy - 1),
        ]

    copies_halo = halo(o_ref, x_halo, y_halo, 0)
    copies_o = gather_band(o_ref, o_far, 0)
    copies_dv = [
        send(dv_ref.at[8 - WIDTH : 8], dvx_halo.at[0], halo_sems, 8, "gx", 1),
        send(dv_ref.at[0:WIDTH], dvx_halo.at[1], halo_sems, 9, "gx", n_gx - 1),
        send(dv_ref, dvy_halo.at[0], halo_sems, 10, "gy", 1),
        send(dv_ref, dvy_halo.at[1], halo_sems, 11, "gy", n_gy - 1),
    ]

    low_x = jnp.where(me["gx"] > 0, 1.0, 0.0).astype(jnp.float32)
    high_x = jnp.where(me["gx"] < n_gx - 1, 1.0, 0.0).astype(jnp.float32)
    low_y = jnp.where(me["gy"] > 0, 1.0, 0.0).astype(jnp.float32)
    high_y = jnp.where(me["gy"] < n_gy - 1, 1.0, 0.0).astype(jnp.float32)

    def weights_of(distance, center):
        out = jnp.where(distance == 0, center, 0.0)
        for k in range(1, 7):
            out = jnp.where(distance == k, taps[k], out)
        return out.astype(jnp.float32)

    za, zb = iota((128, 128), 0), iota((128, 128), 1)
    zd = jnp.abs(za - zb)
    along_z = weights_of(jnp.minimum(zd, 128 - zd), 3.0 * taps[0])
    ra, rb = iota((64, 64), 0), iota((64, 64), 1)
    same = ra // 8 == rb // 8
    ya, yb = ra % 8, rb % 8
    along_y = lanes(
        [
            jnp.where(same, weights_of(ya - (yb - 8), 0.0), 0.0) * low_y,
            jnp.where(same, weights_of(jnp.abs(ya - yb), 0.0), 0.0),
            jnp.where(same, weights_of(yb + 8 - ya, 0.0), 0.0) * high_y,
        ]
    )
    diag = jnp.where(iota((64, 256), 0) % 8 == iota((64, 256), 1) % 8, 1.0, 0.0).astype(jnp.float32)
    fold = jnp.where(iota((256, 128), 0) // 8 == iota((256, 128), 1) % 32, 1.0, 0.0).astype(
        jnp.float32
    )
    unfold = jnp.where(iota((128, 256), 0) % 32 == iota((128, 256), 1) // 8, 1.0, 0.0).astype(
        jnp.float32
    )
    ones = jnp.ones((128, 128), jnp.float32)
    row_n = iota((64, 128), 0) // 8
    lane = iota((64, 128), 1)
    group = jnp.where(lane // 32 == row_n % 4, 1.0, 0.0).astype(jnp.float32)

    levels = rows(
        [jnp.full((8, 128), energies_ref[index_ref[n]], jnp.float32) for n in range(8)]
    )

    def slab(ref, x):
        return ref[:, x].reshape(64, 128)

    def slabs(ref):
        return [slab(ref, x) for x in range(8)]

    def over_bands(plane):
        return rows([plane] * 8)

    def hamiltonian(cur, x_low, x_high, y_low, y_high):
        ny = dot(along_y, rows([lanes(y_low), lanes(cur), lanes(y_high)]))
        nz = dot(rows(cur), along_z)
        line = [x_low[i] * low_x for i in range(6)] + cur + [x_high[i] * high_x for i in range(6)]
        out = []
        for x in range(8):
            total = over_bands(v_ref[x]) * cur[x]
            for k in range(1, 7):
                total = total + taps[k] * (line[x + 6 + k] + line[x + 6 - k])
            out.append(total + ny[:, 128 * x : 128 * x + 128] + nz[64 * x : 64 * x + 64])
        return out

    def stacked(own, far):
        return lanes(
            [
                rows([own[:, x].reshape(64, 128)] + [far[d, :, x].reshape(64, 128) for d in range(n_band - 1)])
                for x in range(8)
            ]
        )

    def intersect(field, everything):
        t = dot_nt(lanes(field), everything) * diag
        s = dot(t, fold) * group
        return rows(
            [jnp.sum(s[0:32], axis=0, keepdims=True), jnp.sum(s[32:64], axis=0, keepdims=True)]
        )

    def dots(pairs):
        parts = []
        for a, b in pairs:
            total = a[0] * b[0]
            for x in range(1, 8):
                total = total + a[x] * b[x]
            parts.append(total)
        stack = rows(parts)
        shape = stack.shape
        total = dot(stack, ones)
        total = jnp.where(iota(shape, 0) // 8 == iota(shape, 1), total, 0.0)
        return jnp.sum(total, axis=0, keepdims=True)

    def pick(row, q):
        return rowsum(jnp.where(lane == row_n + 8 * q, row, 0.0))

    def expand(packed):
        full = rows(
            [jnp.broadcast_to(packed[0:1], (32, 128)), jnp.broadcast_to(packed[1:2], (32, 128))]
        )
        return full * group

    def combine(x_form, everything):
        return dot(dot(x_form, unfold) * diag, everything)

    def split(wide):
        return [wide[:, 128 * x : 128 * x + 128] for x in range(8)]

    def start_sum(src, slots, sems, k, axis):
        n = count[axis]
        order = sorted(range(1, n), key=lambda d: -min(d, n - d))
        for d in order:
            pltpu.make_async_remote_copy(
                src_ref=src,
                dst_ref=slots.at[d - 1],
                send_sem=sems.at[0, k],
                recv_sem=sems.at[1, k],
                device_id=peer(axis, d),
                device_id_type=MESH,
            ).start()

    def finish_sum(src, slots, sems, k):
        pltpu.make_async_copy(slots, slots, sems.at[1, k]).wait()
        total = src[...]
        for d in range(slots.shape[0]):
            total = total + slots[d]
        return total

    def drain(slots, sems, k):
        pltpu.make_async_copy(slots, slots, sems.at[0, k]).wait()

    for copy in copies_halo:
        copy.wait_recv()
    own = slabs(o_ref)
    ox_low, ox_high = ([slab(x_halo.at[side], i) for i in range(WIDTH)] for side in (0, 1))
    oy_low, oy_high = (slabs(y_halo.at[side]) for side in (0, 1))
    ho = hamiltonian(own, ox_low, ox_high, oy_low, oy_high)
    for x in range(8):
        ho_own[:, x] = ho[x].reshape(8, 8, 128)
    copies_ho = gather_band(ho_own, ho_far, n_band - 1)

    for copy in copies_dv:
        copy.wait_recv()
    perturbed = [own[x] * over_bands(dv_ref[x]) for x in range(8)]
    hp = hamiltonian(
        perturbed,
        [ox_low[i] * over_bands(dvx_halo[0, i]) for i in range(WIDTH)],
        [ox_high[i] * over_bands(dvx_halo[1, i]) for i in range(WIDTH)],
        [oy_low[x] * over_bands(dvy_halo[0, x]) for x in range(8)],
        [oy_high[x] * over_bands(dvy_halo[1, x]) for x in range(8)],
    )
    for x in range(8):
        hp_keep[x] = hp[x]

    for copy in copies_o:
        copy.wait_recv()
    orbitals_all = stacked(o_ref, o_far)
    src_g[0, 0:2] = intersect(perturbed, orbitals_all)
    start_sum(src_g.at[0], slots_g.at[0], sum_sems, 0, "gy")

    t = dot_nt(orbitals_all, orbitals_all) * rows([diag] * 4)
    t = dot(t, fold)
    gram = None
    for j in range(4):
        part = jnp.where(lane // 32 == j, t[64 * j : 64 * j + 64], 0.0)
        gram = part if gram is None else gram + part
    gram_src_g[...] = jnp.sum(gram.reshape(8, 8, 128), axis=1)
    start_sum(gram_src_g, gram_slots_g, gram_sems, 0, "gy")

    src_z[0] = finish_sum(src_g.at[0], slots_g.at[0], sum_sems, 0)
    start_sum(src_z.at[0], slots_z.at[0], sum_sems, 1, "gx")
    gram_src_z[...] = finish_sum(gram_src_g, gram_slots_g, gram_sems, 0)
    start_sum(gram_src_z, gram_slots_z, gram_sems, 1, "gx")

    for copy in copies_ho:
        copy.wait_recv()
    ho_all = stacked(ho_own, ho_far)
    total = finish_sum(src_z.at[0], slots_z.at[0], sum_sems, 1)
    x1 = expand(total * (1.0 / cells))
    w1 = dot(x1, unfold) * diag
    o_s1, ho_s1 = split(dot(w1, orbitals_all)), split(dot(w1, ho_all))
    r0 = [o_s1[x] - perturbed[x] for x in range(8)]
    b0 = [ho_s1[x] - hp_keep[x] - levels * r0[x] for x in range(8)]
    for x in range(8):
        b_own[:, x] = b0[x].reshape(8, 8, 128)
    copies_b = halo(b_own, bx_halo, by_halo, 4)

    src_g[1, 0:2] = intersect(b0, orbitals_all)
    src_g[1, 2:3] = dots([(b0, r0), (b0, b0)])
    start_sum(src_g.at[1], slots_g.at[1], sum_sems, 2, "gy")

    gram = finish_sum(gram_src_z, gram_slots_z, gram_sems, 1) * (1.0 / cells)
    turned = [gram] + [pltpu.roll(gram, 32 * k, 1) for k in range(1, 4)]
    lane8 = iota((8, 128), 1)
    gram_blocks = rows(
        [jnp.where(lane8 // 32 == a, turned[(a - j) % 4], 0.0) for a in range(4) for j in range(4)]
    )
    x0 = dot(x1, gram_blocks) - x1
    g0 = dot(x0, gram_blocks)
    w0 = dot(x0, unfold) * diag
    o_s0, ho_s0 = split(dot(w0, orbitals_all)), split(dot(w0, ho_all))

    src_z[1] = finish_sum(src_g.at[1], slots_g.at[1], sum_sems, 2)
    start_sum(src_z.at[1], slots_z.at[1], sum_sems, 3, "gx")

    for copy in copies_b:
        copy.wait_recv()
    lb = hamiltonian(
        b0,
        [slab(bx_halo.at[0], i) for i in range(WIDTH)],
        [slab(bx_halo.at[1], i) for i in range(WIDTH)],
        slabs(by_halo.at[0]),
        slabs(by_halo.at[1]),
    )
    a1 = [b0[x] + level_shift * o_s0[x] for x in range(8)]
    la1 = [
        lb[x] - levels * b0[x] + level_shift * (ho_s0[x] - levels * o_s0[x]) for x in range(8)
    ]

    total = finish_sum(src_z.at[1], slots_z.at[1], sum_sems, 3) * (1.0 / cells)
    xb = expand(total[0:2])
    dots_row = total[2:3]
    numerator = pick(dots_row, 0) + level_shift * rowsum(x0 * x0)
    denominator = pick(dots_row, 1) + rowsum(
        2.0 * level_shift * x0 * xb + (level_shift * level_shift) * x0 * g0
    )
    s1 = numerator / (denominator + epsilon)
    xr = x0 - s1 * (xb + level_shift * g0)
    o_sr = split(combine(xr, orbitals_all))
    r1 = [r0[x] - s1 * a1[x] for x in range(8)]
    ar1 = [b0[x] - s1 * la1[x] + level_shift * o_sr[x] for x in range(8)]

    src_g[2, 0:1] = dots([(ar1, r1), (ar1, ar1)])
    start_sum(src_g.at[2, 0:1], slots_g.at[2, :, 0:1], sum_sems, 4, "gy")
    src_z[2, 0:1] = finish_sum(src_g.at[2, 0:1], slots_g.at[2, :, 0:1], sum_sems, 4)
    start_sum(src_z.at[2, 0:1], slots_z.at[2, :, 0:1], sum_sems, 5, "gx")
    total = finish_sum(src_z.at[2, 0:1], slots_z.at[2, :, 0:1], sum_sems, 5) * (1.0 / cells)
    s2 = pick(total, 0) / (pick(total, 1) + epsilon)

    dens = []
    for x in range(8):
        delta = s1 * r0[x] + s2 * r1[x]
        delta_ref[:, x] = delta.reshape(8, 8, 128)
        dens.append(jnp.sum((delta * own[x]).reshape(8, 8, 128), axis=0))
    shift = lax.rem(128 - 32 * me["band"], 128)
    dens = [pltpu.roll(plane, shift, 1) for plane in dens]
    mine = None
    copies_dens = []
    for d in [2, 1, 3, 0]:
        for half in range(2):
            packed = None
            for j in range(4):
                plane = dens[4 * half + j]
                turn = (32 * (j - d)) % 128
                plane = pltpu.roll(plane, turn, 1) if turn else plane
                packed = plane if packed is None else jnp.where(lane8 // 32 == j, plane, packed)
            dens_src[d, half] = packed
        if d:
            copies_dens.append(send(dens_src.at[d], dens_slots.at[d - 1], dens_sems, d - 1, "band", d))
    for x in range(8):
        residual_ref[:, x] = (r1[x] - s2 * ar1[x]).reshape(8, 8, 128)
    for copy in copies_dens:
        copy.wait_recv()
    for half in range(2):
        total = dens_src[0, half] + dens_slots[0, half] + dens_slots[1, half] + dens_slots[2, half]
        total = total * (4.0 / (8 * n_band))
        for j in range(4):
            plane = pltpu.roll(total, 128 - 32 * j, 1) if j else total
            density_ref[4 * half + j] = plane[:, 0:32]

    for copy in copies_halo + copies_o + copies_dv + copies_ho + copies_b + copies_dens:
        copy.wait_send()
    drain(slots_g.at[0], sum_sems, 0)
    drain(slots_z.at[0], sum_sems, 1)
    drain(slots_g.at[1], sum_sems, 2)
    drain(slots_z.at[1], sum_sems, 3)
    drain(slots_g.at[2, :, 0:1], sum_sems, 4)
    drain(slots_z.at[2, :, 0:1], sum_sems, 5)
    drain(gram_slots_g, gram_sems, 0)
    drain(gram_slots_z, gram_sems, 1)


def shards(sizes, orbitals, delta_potential, potential, energies, band_index):
    n_gx, n_gy, n_band = sizes
    f32 = jnp.float32
    field = (8, 8, 8, 128)
    vmem = pl.BlockSpec(memory_space=pltpu.VMEM)
    smem = pl.BlockSpec(memory_space=pltpu.SMEM)

    def v(*shape):
        return pltpu.VMEM(shape, f32)

    def dma(*shape):
        return pltpu.SemaphoreType.DMA(shape)

    return pl.pallas_call(
        functools.partial(kernel, sizes),
        out_shape=(
            jax.ShapeDtypeStruct(field, f32),
            jax.ShapeDtypeStruct(field, f32),
            jax.ShapeDtypeStruct((8, 8, 128 // n_band), f32),
        ),
        in_specs=[vmem, vmem, vmem, smem, smem],
        out_specs=(vmem, vmem, vmem),
        scratch_shapes=[
            v(n_band - 1, *field),
            v(*field),
            v(n_band - 1, *field),
            v(2, 8, WIDTH, 8, 128),
            v(2, *field),
            v(2, WIDTH, 8, 128),
            v(2, 8, 8, 128),
            v(*field),
            v(2, 8, WIDTH, 8, 128),
            v(2, *field),
            v(8, 64, 128),
            v(3, 3, 128),
            v(3, 3, 128),
            v(3, n_gy - 1, 3, 128),
            v(3, n_gx - 1, 3, 128),
            v(8, 128),
            v(8, 128),
            v(n_gy - 1, 8, 128),
            v(n_gx - 1, 8, 128),
            v(4, 2, 8, 128),
            v(3, 2, 8, 128),
            dma(2, 2 * (n_band - 1)),
            dma(2, 12),
            dma(2, 6),
            dma(2, 2),
            dma(2, 3),
        ],
        compiler_params=pltpu.CompilerParams(
            collective_id=0, has_side_effects=True, vmem_limit_bytes=48 * 2**20
        ),
        name="sternheimer",
    )(orbitals, delta_potential, potential, energies, band_index)


def solution(mesh):
    sizes = tuple(mesh.shape[a] for a in ("gx", "gy", "band"))
    return jax.shard_map(
        functools.partial(shards, sizes),
        mesh=mesh,
        in_specs=(
            P("band", "gx", "gy", None),
            P("gx", "gy", None),
            P("gx", "gy", None),
            P(),
            P("band"),
        ),
        out_specs=(P("band", "gx", "gy", None), P("band", "gx", "gy", None), P("gx", "gy", "band")),
        check_vma=False,
    )
```

```python
import functools

import jax
import jax.numpy as jnp
from jax import lax
from jax.experimental import pallas as pl
from jax.experimental.pallas import tpu as pltpu
from jax.sharding import PartitionSpec as P

stencil_weights = (
    -5369.0 / 1800.0,
    12.0 / 7.0,
    -15.0 / 56.0,
    10.0 / 189.0,
    -1.0 / 112.0,
    2.0 / 1925.0,
    -1.0 / 16632.0,
)
spacing = 0.6
level_shift = 4.0
epsilon = 1e-06
highest = lax.Precision.HIGHEST
scale = -0.5 / (spacing * spacing)
taps = tuple(scale * w for w in stencil_weights)
MESH = pl.DeviceIdType.MESH
WIDTH = 6


def iota(shape, dim):
    return lax.broadcasted_iota(jnp.int32, shape, dim)


def dot(a, b):
    return jnp.dot(a, b, precision=highest, preferred_element_type=jnp.float32)


def dot_nt(a, b):
    return lax.dot_general(
        a, b, (((1,), (1,)), ((), ())), precision=highest, preferred_element_type=jnp.float32
    )


def rowsum(x):
    return jnp.sum(x, axis=1, keepdims=True)


def lanes(parts):
    return jnp.concatenate(parts, axis=1)


def rows(parts):
    return jnp.concatenate(parts, axis=0)


def kernel(
    sizes,
    o_hbm,
    dv_hbm,
    v_hbm,
    energies_hbm,
    index_hbm,
    delta_ref,
    residual_ref,
    density_ref,
    o_all,
    ho_all,
    dv_ref,
    v_ref,
    energies_ref,
    index_ref,
    x_halo,
    y_halo,
    dvx_halo,
    dvy_halo,
    b_own,
    bx_halo,
    by_halo,
    hp_keep,
    src_y,
    slots_y,
    src_g,
    src_z,
    slots_g,
    slots_z,
    gram_all,
    dens_src,
    dens_slots,
    load_sems,
    quarter_sems,
    gather_sems,
    halo_sems,
    sum_sems,
    gram_sems,
    dens_sems,
):
    n_gx, n_gy, n_band = sizes
    me = {a: lax.axis_index(a) for a in ("gx", "gy", "band")}
    count = {"gx": n_gx, "gy": n_gy, "band": n_band}
    cells = float(n_gx * n_gy * 8 * 8 * 128)
    mine = me["band"]

    def peer(axis, offset):
        return {axis: lax.rem(me[axis] + offset, count[axis])}

    loads = [
        pltpu.make_async_copy(src, dst, load_sems.at[i])
        for i, (src, dst) in enumerate(
            [
                (o_hbm, o_all.at[mine]),
                (dv_hbm, dv_ref),
                (v_hbm, v_ref),
                (energies_hbm, energies_ref),
                (index_hbm, index_ref),
            ]
        )
    ]
    for copy in loads:
        copy.start()
    barrier = pltpu.get_barrier_semaphore()
    partners = 0
    for axis in ("gx", "gy", "band"):
        for offset in range(1, count[axis]):
            pl.semaphore_signal(barrier, inc=1, device_id=peer(axis, offset), device_id_type=MESH)
            partners += 1
    for copy in loads:
        copy.wait()
    pl.semaphore_wait(barrier, partners)

    def send(src, dst, sems, k, axis, offset):
        copy = pltpu.make_async_remote_copy(
            src_ref=src,
            dst_ref=dst,
            send_sem=sems.at[0, k],
            recv_sem=sems.at[1, k],
            device_id=peer(axis, offset),
            device_id_type=MESH,
        )
        copy.start()
        return copy

    far = [2, 1, 3]

    def part(x):
        return o_all.at[mine, :, pl.ds(2 * x, 2)]

    copies_quarter = []
    for d in far:
        x = lax.rem(mine + d, 4)
        copies_quarter.append(send(part(x), part(x), quarter_sems, d - 1, "band", d))

    def halo_gx(field, xh, base):
        return [
            send(field.at[:, 8 - WIDTH : 8], xh.at[0], halo_sems, base, "gx", 1),
            send(field.at[:, 0:WIDTH], xh.at[1], halo_sems, base + 1, "gx", n_gx - 1),
        ]

    def halo_gy(field, yh, base):
        return [
            send(field, yh.at[0], halo_sems, base + 2, "gy", 1),
            send(field, yh.at[1], halo_sems, base + 3, "gy", n_gy - 1),
        ]

    copies_halo = halo_gx(o_all.at[mine], x_halo, 0) + halo_gy(o_all.at[mine], y_halo, 0)
    copies_dv = [
        send(dv_ref.at[8 - WIDTH : 8], dvx_halo.at[0], halo_sems, 8, "gx", 1),
        send(dv_ref.at[0:WIDTH], dvx_halo.at[1], halo_sems, 9, "gx", n_gx - 1),
        send(dv_ref, dvy_halo.at[0], halo_sems, 10, "gy", 1),
        send(dv_ref, dvy_halo.at[1], halo_sems, 11, "gy", n_gy - 1),
    ]
    left, right = lax.rem(mine + 3, 4), lax.rem(mine + 1, 4)
    opposite = lax.rem(mine + 2, 4)

    def rows_of(ref, band, start, size):
        return ref.at[band, :, pl.ds(start, size)]

    def pass_on(ref, band, pieces, sems, base, d):
        out = []
        for i, (start, size) in enumerate(pieces):
            piece = rows_of(ref, band, start, size)
            out.append(send(piece, piece, sems, base + i, "band", d))
        return out

    to_right = pass_on(o_all, mine, [(2 * left, 2)], quarter_sems, 3, 1)
    to_left = pass_on(o_all, mine, [(2 * right, 2)], quarter_sems, 7, 3)

    low_x = jnp.where(me["gx"] > 0, 1.0, 0.0).astype(jnp.float32)
    high_x = jnp.where(me["gx"] < n_gx - 1, 1.0, 0.0).astype(jnp.float32)
    low_y = jnp.where(me["gy"] > 0, 1.0, 0.0).astype(jnp.float32)
    high_y = jnp.where(me["gy"] < n_gy - 1, 1.0, 0.0).astype(jnp.float32)

    def weights_of(distance, center):
        out = jnp.where(distance == 0, center, 0.0)
        for k in range(1, 7):
            out = jnp.where(distance == k, taps[k], out)
        return out.astype(jnp.float32)

    za, zb = iota((128, 128), 0), iota((128, 128), 1)
    zd = jnp.abs(za - zb)
    along_z = weights_of(jnp.minimum(zd, 128 - zd), 3.0 * taps[0])
    ra, rb = iota((64, 64), 0), iota((64, 64), 1)
    same = ra // 8 == rb // 8
    ya, yb = ra % 8, rb % 8
    along_y = lanes(
        [
            jnp.where(same, weights_of(ya - (yb - 8), 0.0), 0.0) * low_y,
            jnp.where(same, weights_of(jnp.abs(ya - yb), 0.0), 0.0),
            jnp.where(same, weights_of(yb + 8 - ya, 0.0), 0.0) * high_y,
        ]
    )
    diag = jnp.where(iota((64, 256), 0) % 8 == iota((64, 256), 1) % 8, 1.0, 0.0).astype(jnp.float32)
    fold = jnp.where(iota((256, 128), 0) // 8 == iota((256, 128), 1) % 32, 1.0, 0.0).astype(
        jnp.float32
    )
    unfold = jnp.where(iota((128, 256), 0) % 32 == iota((128, 256), 1) // 8, 1.0, 0.0).astype(
        jnp.float32
    )
    ones = jnp.ones((128, 128), jnp.float32)
    row_n = iota((64, 128), 0) // 8
    lane = iota((64, 128), 1)
    group = jnp.where(lane // 32 == row_n % 4, 1.0, 0.0).astype(jnp.float32)

    levels = rows(
        [jnp.full((8, 128), energies_ref[index_ref[n]], jnp.float32) for n in range(8)]
    )

    def slab(ref, x):
        return ref[:, x].reshape(64, 128)

    def slabs(ref):
        return [slab(ref, x) for x in range(8)]

    def over_bands(plane):
        return rows([plane] * 8)

    def hamiltonian(cur, x_low, x_high, y_low, y_high):
        ny = dot(along_y, rows([lanes(y_low), lanes(cur), lanes(y_high)]))
        nz = dot(rows(cur), along_z)
        line = [x_low[i] * low_x for i in range(6)] + cur + [x_high[i] * high_x for i in range(6)]
        out = []
        for x in range(8):
            total = over_bands(v_ref[x]) * cur[x]
            for k in range(1, 7):
                total = total + taps[k] * (line[x + 6 + k] + line[x + 6 - k])
            out.append(total + ny[:, 128 * x : 128 * x + 128] + nz[64 * x : 64 * x + 64])
        return out

    def column(ref, x):
        return rows([ref[q, :, x].reshape(64, 128) for q in range(4)])

    def stacked(ref):
        return lanes([column(ref, x) for x in range(8)])

    def packed(t):
        t = t * group
        return rows(
            [jnp.sum(t[0:32], axis=0, keepdims=True), jnp.sum(t[32:64], axis=0, keepdims=True)]
        )

    def intersect(field, everything):
        return packed(dot(dot_nt(lanes(field), everything) * diag, fold))

    def dots(pairs):
        parts = []
        for a, b in pairs:
            total = a[0] * b[0]
            for x in range(1, 8):
                total = total + a[x] * b[x]
            parts.append(total)
        stack = rows(parts)
        shape = stack.shape
        total = dot(stack, ones)
        total = jnp.where(iota(shape, 0) // 8 == iota(shape, 1), total, 0.0)
        return jnp.sum(total, axis=0, keepdims=True)

    def pick(row, q):
        return rowsum(jnp.where(lane == row_n + 8 * q, row, 0.0))

    def expand(packed):
        full = rows(
            [jnp.broadcast_to(packed[0:1], (32, 128)), jnp.broadcast_to(packed[1:2], (32, 128))]
        )
        return full * group

    def combine(x_form, everything):
        return dot(dot(x_form, unfold) * diag, everything)

    def split(wide):
        return [wide[:, 128 * x : 128 * x + 128] for x in range(8)]

    def start_sum(src, slots, k, axis):
        n = count[axis]
        sems = sum_sems
        order = sorted(range(1, n), key=lambda d: -min(d, n - d))
        for d in order:
            pltpu.make_async_remote_copy(
                src_ref=src,
                dst_ref=slots.at[d - 1],
                send_sem=sems.at[0, k],
                recv_sem=sems.at[1, k],
                device_id=peer(axis, d),
                device_id_type=MESH,
            ).start()

    def finish_sum(src, slots, k):
        pltpu.make_async_copy(slots, slots, sum_sems.at[1, k]).wait()
        total = src[...]
        for d in range(slots.shape[0]):
            total = total + slots[d]
        return total

    def drain(slots, k):
        pltpu.make_async_copy(slots, slots, sum_sems.at[0, k]).wait()

    for copy in copies_quarter:
        copy.wait_recv()
    pieces, pieces_p = [], []
    for i in range(2):
        piece = column(o_all, 2 * mine + i)
        pieces.append(piece)
        pieces_p.append(piece * rows([dv_ref[2 * mine + i]] * 32))
    quarter = lanes(pieces)
    t = dot_nt(rows([lanes(pieces_p), quarter]), quarter) * rows([diag] * 8)
    t = dot(t, fold)
    for q in range(4):
        src_y[q, 0:2] = packed(t[64 * q : 64 * q + 64])
        src_y[q, 2:4] = packed(t[256 + 64 * q : 256 + 64 * q + 64])
    copies_y = [
        send(src_y.at[lax.rem(mine + d, 4)], slots_y.at[d - 1], gram_sems, d - 1, "band", d)
        for d in far
    ]

    low, high = (2 * mine, 1), (2 * mine + 1, 1)
    to_right += pass_on(o_all, mine, [low, high, (2 * opposite, 2)], quarter_sems, 4, 1)
    to_left += pass_on(o_all, mine, [high, low, (2 * opposite, 2)], quarter_sems, 8, 3)

    for copy in copies_halo:
        copy.wait_recv()
    own = slabs(o_all.at[mine])
    ox_low, ox_high = ([slab(x_halo.at[side], i) for i in range(WIDTH)] for side in (0, 1))
    oy_low, oy_high = (slabs(y_halo.at[side]) for side in (0, 1))
    ho = hamiltonian(own, ox_low, ox_high, oy_low, oy_high)
    for x in range(8):
        ho_all[mine, :, x] = ho[x].reshape(8, 8, 128)
    for copy in copies_y:
        copy.wait_recv()
    src_g[0] = src_y[mine] + slots_y[0] + slots_y[1] + slots_y[2]
    start_sum(src_g.at[0], slots_g.at[0], 0, "gy")

    for copy in to_right[:2] + to_left[:2]:
        copy.wait_recv()
    onward = pass_on(o_all, left, [(2 * opposite, 2), (2 * left, 1)], quarter_sems, 11, 1)
    onward += pass_on(o_all, right, [(2 * opposite, 2), (2 * right + 1, 1)], quarter_sems, 13, 3)
    copies_o = to_right + to_left + onward
    ho_right = pass_on(ho_all, mine, [(0, 4), (4, 4)], gather_sems, 0, 1)
    ho_left = pass_on(ho_all, mine, [(4, 4), (0, 4)], gather_sems, 2, 3)

    for copy in copies_dv:
        copy.wait_recv()
    perturbed = [own[x] * over_bands(dv_ref[x]) for x in range(8)]
    hp = hamiltonian(
        perturbed,
        [ox_low[i] * over_bands(dvx_halo[0, i]) for i in range(WIDTH)],
        [ox_high[i] * over_bands(dvx_halo[1, i]) for i in range(WIDTH)],
        [oy_low[x] * over_bands(dvy_halo[0, x]) for x in range(8)],
        [oy_high[x] * over_bands(dvy_halo[1, x]) for x in range(8)],
    )
    for x in range(8):
        hp_keep[x] = hp[x]

    src_z[0] = finish_sum(src_g.at[0], slots_g.at[0], 0)
    start_sum(src_z.at[0], slots_z.at[0], 1, "gx")

    for copy in [ho_right[0], ho_left[0]]:
        copy.wait_recv()
    copies_ho = ho_right + ho_left
    copies_ho += pass_on(ho_all, left, [(0, 4)], gather_sems, 4, 1)
    copies_ho += pass_on(ho_all, right, [(4, 4)], gather_sems, 5, 3)
    for copy in to_right[2:] + to_left[2:] + onward:
        copy.wait_recv()
    orbitals_all = stacked(o_all)
    total = finish_sum(src_z.at[0], slots_z.at[0], 1) * (1.0 / cells)
    gram_all[mine] = total[2:4]
    copies_gram = [
        send(gram_all.at[mine], gram_all.at[mine], gram_sems, 2 + d, "band", d) for d in far
    ]
    for copy in ho_right[1:] + ho_left[1:] + copies_ho[4:]:
        copy.wait_recv()
    h_orbitals_all = stacked(ho_all)
    x1 = expand(total[0:2])
    w1 = dot(x1, unfold) * diag
    o_s1, ho_s1 = split(dot(w1, orbitals_all)), split(dot(w1, h_orbitals_all))
    r0 = [o_s1[x] - perturbed[x] for x in range(8)]
    b0 = [ho_s1[x] - hp_keep[x] - levels * r0[x] for x in range(8)]
    for x in range(8):
        b_own[:, x] = b0[x].reshape(8, 8, 128)
    copies_b = halo_gx(b_own, bx_halo, 4)

    src_g[1, 0:2] = intersect(b0, orbitals_all)
    src_g[1, 2:3] = dots([(b0, r0), (b0, b0)])
    start_sum(src_g.at[1, 0:3], slots_g.at[1, :, 0:3], 2, "gy")
    copies_b += halo_gy(b_own, by_halo, 4)

    for copy in copies_gram:
        copy.wait_recv()
    gram = rows([jnp.broadcast_to(gram_all[q, r : r + 1], (8, 128)) for q in range(4) for r in range(2)])
    pick_rows = jnp.where(
        iota((32, 64), 1) == 8 * (iota((32, 64), 0) // 4), 1.0, 0.0
    ).astype(jnp.float32)
    gram = jnp.where(iota((32, 128), 1) // 32 == iota((32, 128), 0) % 4, dot(pick_rows, gram), 0.0)
    repeat = jnp.where(iota((128, 128), 0) % 32 == iota((128, 128), 1) % 32, 1.0, 0.0).astype(
        jnp.float32
    )
    gram = dot(gram, repeat)
    gram_blocks = jnp.where(
        iota((128, 128), 0) // 32 == iota((128, 128), 1) // 32, rows([gram] * 4), 0.0
    )
    x0 = dot(x1, gram_blocks) - x1
    g0 = dot(x0, gram_blocks)
    w0 = dot(x0, unfold) * diag
    o_s0, ho_s0 = split(dot(w0, orbitals_all)), split(dot(w0, h_orbitals_all))

    src_z[1, 0:3] = finish_sum(src_g.at[1, 0:3], slots_g.at[1, :, 0:3], 2)
    start_sum(src_z.at[1, 0:3], slots_z.at[1, :, 0:3], 3, "gx")

    for copy in copies_b:
        copy.wait_recv()
    lb = hamiltonian(
        b0,
        [slab(bx_halo.at[0], i) for i in range(WIDTH)],
        [slab(bx_halo.at[1], i) for i in range(WIDTH)],
        slabs(by_halo.at[0]),
        slabs(by_halo.at[1]),
    )
    a1 = [b0[x] + level_shift * o_s0[x] for x in range(8)]
    la1 = [
        lb[x] - levels * b0[x] + level_shift * (ho_s0[x] - levels * o_s0[x]) for x in range(8)
    ]

    total = finish_sum(src_z.at[1, 0:3], slots_z.at[1, :, 0:3], 3) * (1.0 / cells)
    xb = expand(total[0:2])
    dots_row = total[2:3]
    numerator = pick(dots_row, 0) + level_shift * rowsum(x0 * x0)
    denominator = pick(dots_row, 1) + rowsum(
        2.0 * level_shift * x0 * xb + (level_shift * level_shift) * x0 * g0
    )
    s1 = numerator / (denominator + epsilon)
    xr = x0 - s1 * (xb + level_shift * g0)
    o_sr = split(combine(xr, orbitals_all))
    r1 = [r0[x] - s1 * a1[x] for x in range(8)]
    ar1 = [b0[x] - s1 * la1[x] + level_shift * o_sr[x] for x in range(8)]

    src_g[2, 0:1] = dots([(ar1, r1), (ar1, ar1)])
    start_sum(src_g.at[2, 0:1], slots_g.at[2, :, 0:1], 4, "gy")
    src_z[2, 0:1] = finish_sum(src_g.at[2, 0:1], slots_g.at[2, :, 0:1], 4)
    start_sum(src_z.at[2, 0:1], slots_z.at[2, :, 0:1], 5, "gx")
    total = finish_sum(src_z.at[2, 0:1], slots_z.at[2, :, 0:1], 5) * (1.0 / cells)
    s2 = pick(total, 0) / (pick(total, 1) + epsilon)

    dens = []
    for x in range(8):
        delta = s1 * r0[x] + s2 * r1[x]
        delta_ref[:, x] = delta.reshape(8, 8, 128)
        dens.append(jnp.sum((delta * own[x]).reshape(8, 8, 128), axis=0))
    shift = lax.rem(128 - 32 * me["band"], 128)
    dens = [pltpu.roll(plane, shift, 1) for plane in dens]
    copies_dens = []
    lane8 = iota((8, 128), 1)
    for d in [2, 1, 3, 0]:
        for half in range(2):
            packed = None
            for j in range(4):
                plane = dens[4 * half + j]
                turn = (32 * (j - d)) % 128
                plane = pltpu.roll(plane, turn, 1) if turn else plane
                packed = plane if packed is None else jnp.where(lane8 // 32 == j, plane, packed)
            dens_src[d, half] = packed
        if d:
            copies_dens.append(send(dens_src.at[d], dens_slots.at[d - 1], dens_sems, d - 1, "band", d))
    for x in range(8):
        residual_ref[:, x] = (r1[x] - s2 * ar1[x]).reshape(8, 8, 128)
    for copy in copies_dens:
        copy.wait_recv()
    for half in range(2):
        total = dens_src[0, half] + dens_slots[0, half] + dens_slots[1, half] + dens_slots[2, half]
        total = total * (4.0 / (8 * n_band))
        for j in range(4):
            plane = pltpu.roll(total, 128 - 32 * j, 1) if j else total
            density_ref[4 * half + j] = plane[:, 0:32]

    for copy in (
        copies_quarter + copies_o + copies_halo + copies_dv + copies_y + copies_ho + copies_gram + copies_b + copies_dens
    ):
        copy.wait_send()
    drain(slots_g.at[0], 0)
    drain(slots_z.at[0], 1)
    drain(slots_g.at[1, :, 0:3], 2)
    drain(slots_z.at[1, :, 0:3], 3)
    drain(slots_g.at[2, :, 0:1], 4)
    drain(slots_z.at[2, :, 0:1], 5)


def shards(sizes, orbitals, delta_potential, potential, energies, band_index):
    n_gx, n_gy, n_band = sizes
    f32 = jnp.float32
    field = (8, 8, 8, 128)
    vmem = pl.BlockSpec(memory_space=pltpu.VMEM)
    hbm = pl.BlockSpec(memory_space=pltpu.HBM)

    def v(*shape):
        return pltpu.VMEM(shape, f32)

    def dma(*shape):
        return pltpu.SemaphoreType.DMA(shape)

    outs = (
        jax.ShapeDtypeStruct(field, f32),
        jax.ShapeDtypeStruct(field, f32),
        jax.ShapeDtypeStruct((8, 8, 128 // n_band), f32),
    )
    return pl.pallas_call(
        functools.partial(kernel, sizes),
        out_shape=outs,
        in_specs=[hbm] * 5,
        out_specs=(vmem, vmem, vmem),
        scratch_shapes=[
            v(4, *field),
            v(4, *field),
            v(8, 8, 128),
            v(8, 8, 128),
            pltpu.SMEM(energies.shape, f32),
            pltpu.SMEM(band_index.shape, jnp.int32),
            v(2, 8, WIDTH, 8, 128),
            v(2, *field),
            v(2, WIDTH, 8, 128),
            v(2, 8, 8, 128),
            v(*field),
            v(2, 8, WIDTH, 8, 128),
            v(2, *field),
            v(8, 64, 128),
            v(4, 4, 128),
            v(3, 4, 128),
            v(3, 4, 128),
            v(3, 4, 128),
            v(3, n_gy - 1, 4, 128),
            v(3, n_gx - 1, 4, 128),
            v(4, 2, 128),
            v(4, 2, 8, 128),
            v(3, 2, 8, 128),
            dma(5),
            dma(2, 15),
            dma(2, 6),
            dma(2, 12),
            dma(2, 6),
            dma(2, 6),
            dma(2, 3),
        ],
        compiler_params=pltpu.CompilerParams(
            collective_id=0, has_side_effects=True, vmem_limit_bytes=48 * 2**20
        ),
        name="sternheimer",
    )(
        *[
            pltpu.with_memory_space_constraint(a, pltpu.HBM)
            for a in (orbitals, delta_potential, potential, energies, band_index)
        ]
    )

def solution(mesh):
    sizes = tuple(mesh.shape[a] for a in ("gx", "gy", "band"))
    return jax.shard_map(
        functools.partial(shards, sizes),
        mesh=mesh,
        in_specs=(
            P("band", "gx", "gy", None),
            P("gx", "gy", None),
            P("gx", "gy", None),
            P(),
            P("band"),
        ),
        out_specs=(P("band", "gx", "gy", None), P("band", "gx", "gy", None), P("gx", "gy", "band")),
        check_vma=False,
    )
```

```python
import functools

import jax
import jax.numpy as jnp
from jax import lax
from jax.experimental import pallas as pl
from jax.experimental.pallas import tpu as pltpu
from jax.sharding import PartitionSpec as P

stencil_weights = (
    -5369.0 / 1800.0,
    12.0 / 7.0,
    -15.0 / 56.0,
    10.0 / 189.0,
    -1.0 / 112.0,
    2.0 / 1925.0,
    -1.0 / 16632.0,
)
spacing = 0.6
level_shift = 4.0
epsilon = 1e-06
highest = lax.Precision.HIGHEST
scale = -0.5 / (spacing * spacing)
taps = tuple(scale * w for w in stencil_weights)
MESH = pl.DeviceIdType.MESH
WIDTH = 6


def iota(shape, dim):
    return lax.broadcasted_iota(jnp.int32, shape, dim)


def dot(a, b):
    return jnp.dot(a, b, precision=highest, preferred_element_type=jnp.float32)


def dot_nt(a, b):
    return lax.dot_general(
        a, b, (((1,), (1,)), ((), ())), precision=highest, preferred_element_type=jnp.float32
    )


def rowsum(x):
    return jnp.sum(x, axis=1, keepdims=True)


def lanes(parts):
    return jnp.concatenate(parts, axis=1)


def rows(parts):
    return jnp.concatenate(parts, axis=0)


def kernel(
    sizes,
    o_hbm,
    dv_hbm,
    v_hbm,
    energies_hbm,
    index_hbm,
    delta_ref,
    residual_ref,
    density_ref,
    o_all,
    ho_all,
    dv_ref,
    v_ref,
    energies_ref,
    index_ref,
    x_halo,
    y_halo,
    dvx_halo,
    dvy_halo,
    b_own,
    bx_halo,
    by_halo,
    hp_keep,
    src_y,
    slots_y,
    src_g,
    src_z,
    slots_g,
    slots_z,
    gram_all,
    dens_src,
    dens_slots,
    load_sems,
    relay_sems,
    quarter_sems,
    gather_sems,
    halo_sems,
    sum_sems,
    gram_sems,
    dens_sems,
):
    n_gx, n_gy, n_band = sizes
    me = {a: lax.axis_index(a) for a in ("gx", "gy", "band")}
    count = {"gx": n_gx, "gy": n_gy, "band": n_band}
    cells = float(n_gx * n_gy * 8 * 8 * 128)
    mine = me["band"]

    def peer(axis, offset):
        return {axis: lax.rem(me[axis] + offset, count[axis])}

    loads = [
        pltpu.make_async_copy(src, dst, load_sems.at[i])
        for i, (src, dst) in enumerate(
            [
                (o_hbm, o_all.at[mine]),
                (dv_hbm, dv_ref),
                (v_hbm, v_ref),
                (energies_hbm, energies_ref),
                (index_hbm, index_ref),
            ]
        )
    ]
    for copy in loads:
        copy.start()
    barrier = pltpu.get_barrier_semaphore()
    partners = 0
    sides = (1, n_gx - 1)
    for axis, offsets in (("gx", sides), ("gy", range(1, n_gy)), ("band", range(1, n_band))):
        for offset in offsets:
            pl.semaphore_signal(barrier, inc=1, device_id=peer(axis, offset), device_id_type=MESH)
            partners += 1
    for copy in loads:
        copy.wait()
    pl.semaphore_wait(barrier, partners)

    def send(src, dst, sems, k, axis, offset):
        copy = pltpu.make_async_remote_copy(
            src_ref=src,
            dst_ref=dst,
            send_sem=sems.at[0, k],
            recv_sem=sems.at[1, k],
            device_id=peer(axis, offset),
            device_id_type=MESH,
        )
        copy.start()
        return copy

    def tell(step):
        for offset in (2**step, n_gx - 2**step):
            pl.semaphore_signal(
                relay_sems.at[step], inc=1, device_id=peer("gx", offset), device_id_type=MESH
            )

    def hear(step):
        pl.semaphore_wait(relay_sems.at[step], 2)

    far = [2, 1, 3]

    def part(x):
        return o_all.at[mine, :, pl.ds(2 * x, 2)]

    copies_quarter = []
    for d in far:
        x = lax.rem(mine + d, 4)
        copies_quarter.append(send(part(x), part(x), quarter_sems, d - 1, "band", d))

    def halo_gx(field, xh, base):
        return [
            send(field.at[:, 8 - WIDTH : 8], xh.at[0], halo_sems, base, "gx", 1),
            send(field.at[:, 0:WIDTH], xh.at[1], halo_sems, base + 1, "gx", n_gx - 1),
        ]

    def halo_gy(field, yh, base):
        return [
            send(field, yh.at[0], halo_sems, base + 2, "gy", 1),
            send(field, yh.at[1], halo_sems, base + 3, "gy", n_gy - 1),
        ]

    copies_halo = halo_gx(o_all.at[mine], x_halo, 0) + halo_gy(o_all.at[mine], y_halo, 0)
    copies_dv = [
        send(dv_ref.at[8 - WIDTH : 8], dvx_halo.at[0], halo_sems, 8, "gx", 1),
        send(dv_ref.at[0:WIDTH], dvx_halo.at[1], halo_sems, 9, "gx", n_gx - 1),
        send(dv_ref, dvy_halo.at[0], halo_sems, 10, "gy", 1),
        send(dv_ref, dvy_halo.at[1], halo_sems, 11, "gy", n_gy - 1),
    ]
    left, right = lax.rem(mine + 3, 4), lax.rem(mine + 1, 4)
    opposite = lax.rem(mine + 2, 4)

    def rows_of(ref, band, start, size):
        return ref.at[band, :, pl.ds(start, size)]

    def pass_on(ref, band, pieces, sems, base, d):
        out = []
        for i, (start, size) in enumerate(pieces):
            piece = rows_of(ref, band, start, size)
            out.append(send(piece, piece, sems, base + i, "band", d))
        return out

    to_right = pass_on(o_all, mine, [(2 * left, 2)], quarter_sems, 3, 1)
    to_left = pass_on(o_all, mine, [(2 * right, 2)], quarter_sems, 7, 3)

    tell(0)

    low_x = jnp.where(me["gx"] > 0, 1.0, 0.0).astype(jnp.float32)
    high_x = jnp.where(me["gx"] < n_gx - 1, 1.0, 0.0).astype(jnp.float32)
    low_y = jnp.where(me["gy"] > 0, 1.0, 0.0).astype(jnp.float32)
    high_y = jnp.where(me["gy"] < n_gy - 1, 1.0, 0.0).astype(jnp.float32)

    def weights_of(distance, center):
        out = jnp.where(distance == 0, center, 0.0)
        for k in range(1, 7):
            out = jnp.where(distance == k, taps[k], out)
        return out.astype(jnp.float32)

    za, zb = iota((128, 128), 0), iota((128, 128), 1)
    zd = jnp.abs(za - zb)
    along_z = weights_of(jnp.minimum(zd, 128 - zd), 3.0 * taps[0])
    ra, rb = iota((64, 64), 0), iota((64, 64), 1)
    same = ra // 8 == rb // 8
    ya, yb = ra % 8, rb % 8
    along_y = lanes(
        [
            jnp.where(same, weights_of(ya - (yb - 8), 0.0), 0.0) * low_y,
            jnp.where(same, weights_of(jnp.abs(ya - yb), 0.0), 0.0),
            jnp.where(same, weights_of(yb + 8 - ya, 0.0), 0.0) * high_y,
        ]
    )
    diag = jnp.where(iota((64, 256), 0) % 8 == iota((64, 256), 1) % 8, 1.0, 0.0).astype(jnp.float32)
    fold = jnp.where(iota((256, 128), 0) // 8 == iota((256, 128), 1) % 32, 1.0, 0.0).astype(
        jnp.float32
    )
    unfold = jnp.where(iota((128, 256), 0) % 32 == iota((128, 256), 1) // 8, 1.0, 0.0).astype(
        jnp.float32
    )
    ones = jnp.ones((128, 128), jnp.float32)
    row_n = iota((64, 128), 0) // 8
    lane = iota((64, 128), 1)
    group = jnp.where(lane // 32 == row_n % 4, 1.0, 0.0).astype(jnp.float32)

    levels = rows(
        [jnp.full((8, 128), energies_ref[index_ref[n]], jnp.float32) for n in range(8)]
    )

    def slab(ref, x):
        return ref[:, x].reshape(64, 128)

    def slabs(ref):
        return [slab(ref, x) for x in range(8)]

    def over_bands(plane):
        return rows([plane] * 8)

    def hamiltonian(cur, x_low, x_high, y_low, y_high):
        ny = dot(along_y, rows([lanes(y_low), lanes(cur), lanes(y_high)]))
        nz = dot(rows(cur), along_z)
        line = [x_low[i] * low_x for i in range(6)] + cur + [x_high[i] * high_x for i in range(6)]
        out = []
        for x in range(8):
            total = over_bands(v_ref[x]) * cur[x]
            for k in range(1, 7):
                total = total + taps[k] * (line[x + 6 + k] + line[x + 6 - k])
            out.append(total + ny[:, 128 * x : 128 * x + 128] + nz[64 * x : 64 * x + 64])
        return out

    def column(ref, x):
        return rows([ref[q, :, x].reshape(64, 128) for q in range(4)])

    def stacked(ref):
        return lanes([column(ref, x) for x in range(8)])

    def packed(t):
        t = t * group
        return rows(
            [jnp.sum(t[0:32], axis=0, keepdims=True), jnp.sum(t[32:64], axis=0, keepdims=True)]
        )

    def intersect(field, everything):
        return packed(dot(dot_nt(lanes(field), everything) * diag, fold))

    def dots(pairs):
        parts = []
        for a, b in pairs:
            total = a[0] * b[0]
            for x in range(1, 8):
                total = total + a[x] * b[x]
            parts.append(total)
        stack = rows(parts)
        shape = stack.shape
        total = dot(stack, ones)
        total = jnp.where(iota(shape, 0) // 8 == iota(shape, 1), total, 0.0)
        return jnp.sum(total, axis=0, keepdims=True)

    def pick(row, q):
        return rowsum(jnp.where(lane == row_n + 8 * q, row, 0.0))

    def expand(packed):
        full = rows(
            [jnp.broadcast_to(packed[0:1], (32, 128)), jnp.broadcast_to(packed[1:2], (32, 128))]
        )
        return full * group

    def combine(x_form, everything):
        return dot(dot(x_form, unfold) * diag, everything)

    def split(wide):
        return [wide[:, 128 * x : 128 * x + 128] for x in range(8)]

    def start_sum(src, slots, k, axis):
        n = count[axis]
        sems = sum_sems
        order = sorted(range(1, n), key=lambda d: -min(d, n - d))
        for d in order:
            pltpu.make_async_remote_copy(
                src_ref=src,
                dst_ref=slots.at[d - 1],
                send_sem=sems.at[0, k],
                recv_sem=sems.at[1, k],
                device_id=peer(axis, d),
                device_id_type=MESH,
            ).start()

    def finish_sum(src, slots, k):
        pltpu.make_async_copy(slots, slots, sum_sems.at[1, k]).wait()
        total = src[...]
        for d in range(slots.shape[0]):
            total = total + slots[d]
        return total

    def drain(slots, k):
        pltpu.make_async_copy(slots, slots, sum_sems.at[0, k]).wait()

    hear(0)
    tell(1)
    for copy in copies_quarter:
        copy.wait_recv()
    pieces, pieces_p = [], []
    for i in range(2):
        piece = column(o_all, 2 * mine + i)
        pieces.append(piece)
        pieces_p.append(piece * rows([dv_ref[2 * mine + i]] * 32))
    quarter = lanes(pieces)
    t = dot_nt(rows([lanes(pieces_p), quarter]), quarter) * rows([diag] * 8)
    t = dot(t, fold)
    for q in range(4):
        src_y[q, 0:2] = packed(t[64 * q : 64 * q + 64])
        src_y[q, 2:4] = packed(t[256 + 64 * q : 256 + 64 * q + 64])
    copies_y = [
        send(src_y.at[lax.rem(mine + d, 4)], slots_y.at[d - 1], gram_sems, d - 1, "band", d)
        for d in far
    ]

    low, high = (2 * mine, 1), (2 * mine + 1, 1)
    to_right += pass_on(o_all, mine, [low, high, (2 * opposite, 2)], quarter_sems, 4, 1)
    to_left += pass_on(o_all, mine, [high, low, (2 * opposite, 2)], quarter_sems, 8, 3)

    for copy in copies_halo:
        copy.wait_recv()
    own = slabs(o_all.at[mine])
    ox_low, ox_high = ([slab(x_halo.at[side], i) for i in range(WIDTH)] for side in (0, 1))
    oy_low, oy_high = (slabs(y_halo.at[side]) for side in (0, 1))
    ho = hamiltonian(own, ox_low, ox_high, oy_low, oy_high)
    for x in range(8):
        ho_all[mine, :, x] = ho[x].reshape(8, 8, 128)
    hear(1)
    tell(2)
    for copy in copies_y:
        copy.wait_recv()
    src_g[0] = src_y[mine] + slots_y[0] + slots_y[1] + slots_y[2]
    start_sum(src_g.at[0], slots_g.at[0], 0, "gy")

    for copy in to_right[:2] + to_left[:2]:
        copy.wait_recv()
    onward = pass_on(o_all, left, [(2 * opposite, 2), (2 * left, 1)], quarter_sems, 11, 1)
    onward += pass_on(o_all, right, [(2 * opposite, 2), (2 * right + 1, 1)], quarter_sems, 13, 3)
    copies_o = to_right + to_left + onward
    ho_right = pass_on(ho_all, mine, [(0, 4), (4, 4)], gather_sems, 0, 1)
    ho_left = pass_on(ho_all, mine, [(4, 4), (0, 4)], gather_sems, 2, 3)

    for copy in copies_dv:
        copy.wait_recv()
    perturbed = [own[x] * over_bands(dv_ref[x]) for x in range(8)]
    hp = hamiltonian(
        perturbed,
        [ox_low[i] * over_bands(dvx_halo[0, i]) for i in range(WIDTH)],
        [ox_high[i] * over_bands(dvx_halo[1, i]) for i in range(WIDTH)],
        [oy_low[x] * over_bands(dvy_halo[0, x]) for x in range(8)],
        [oy_high[x] * over_bands(dvy_halo[1, x]) for x in range(8)],
    )
    for x in range(8):
        hp_keep[x] = hp[x]

    hear(2)
    src_z[0] = finish_sum(src_g.at[0], slots_g.at[0], 0)
    start_sum(src_z.at[0], slots_z.at[0], 1, "gx")

    for copy in [ho_right[0], ho_left[0]]:
        copy.wait_recv()
    copies_ho = ho_right + ho_left
    copies_ho += pass_on(ho_all, left, [(0, 4)], gather_sems, 4, 1)
    copies_ho += pass_on(ho_all, right, [(4, 4)], gather_sems, 5, 3)
    for copy in to_right[2:] + to_left[2:] + onward:
        copy.wait_recv()
    orbitals_all = stacked(o_all)
    total = finish_sum(src_z.at[0], slots_z.at[0], 1) * (1.0 / cells)
    gram_all[mine] = total[2:4]
    copies_gram = [
        send(gram_all.at[mine], gram_all.at[mine], gram_sems, 2 + d, "band", d) for d in far
    ]
    for copy in ho_right[1:] + ho_left[1:] + copies_ho[4:]:
        copy.wait_recv()
    h_orbitals_all = stacked(ho_all)
    x1 = expand(total[0:2])
    w1 = dot(x1, unfold) * diag
    o_s1, ho_s1 = split(dot(w1, orbitals_all)), split(dot(w1, h_orbitals_all))
    r0 = [o_s1[x] - perturbed[x] for x in range(8)]
    b0 = [ho_s1[x] - hp_keep[x] - levels * r0[x] for x in range(8)]
    for x in range(8):
        b_own[:, x] = b0[x].reshape(8, 8, 128)
    copies_b = halo_gx(b_own, bx_halo, 4)

    src_g[1, 0:2] = intersect(b0, orbitals_all)
    src_g[1, 2:3] = dots([(b0, r0), (b0, b0)])
    start_sum(src_g.at[1, 0:3], slots_g.at[1, :, 0:3], 2, "gy")
    copies_b += halo_gy(b_own, by_halo, 4)

    for copy in copies_gram:
        copy.wait_recv()
    gram = rows([jnp.broadcast_to(gram_all[q, r : r + 1], (8, 128)) for q in range(4) for r in range(2)])
    pick_rows = jnp.where(
        iota((32, 64), 1) == 8 * (iota((32, 64), 0) // 4), 1.0, 0.0
    ).astype(jnp.float32)
    gram = jnp.where(iota((32, 128), 1) // 32 == iota((32, 128), 0) % 4, dot(pick_rows, gram), 0.0)
    repeat = jnp.where(iota((128, 128), 0) % 32 == iota((128, 128), 1) % 32, 1.0, 0.0).astype(
        jnp.float32
    )
    gram = dot(gram, repeat)
    gram_blocks = jnp.where(
        iota((128, 128), 0) // 32 == iota((128, 128), 1) // 32, rows([gram] * 4), 0.0
    )
    x0 = dot(x1, gram_blocks) - x1
    g0 = dot(x0, gram_blocks)
    w0 = dot(x0, unfold) * diag
    o_s0, ho_s0 = split(dot(w0, orbitals_all)), split(dot(w0, h_orbitals_all))

    src_z[1, 0:3] = finish_sum(src_g.at[1, 0:3], slots_g.at[1, :, 0:3], 2)
    start_sum(src_z.at[1, 0:3], slots_z.at[1, :, 0:3], 3, "gx")

    for copy in copies_b:
        copy.wait_recv()
    lb = hamiltonian(
        b0,
        [slab(bx_halo.at[0], i) for i in range(WIDTH)],
        [slab(bx_halo.at[1], i) for i in range(WIDTH)],
        slabs(by_halo.at[0]),
        slabs(by_halo.at[1]),
    )
    a1 = [b0[x] + level_shift * o_s0[x] for x in range(8)]
    la1 = [
        lb[x] - levels * b0[x] + level_shift * (ho_s0[x] - levels * o_s0[x]) for x in range(8)
    ]

    total = finish_sum(src_z.at[1, 0:3], slots_z.at[1, :, 0:3], 3) * (1.0 / cells)
    xb = expand(total[0:2])
    dots_row = total[2:3]
    numerator = pick(dots_row, 0) + level_shift * rowsum(x0 * x0)
    denominator = pick(dots_row, 1) + rowsum(
        2.0 * level_shift * x0 * xb + (level_shift * level_shift) * x0 * g0
    )
    s1 = numerator / (denominator + epsilon)
    xr = x0 - s1 * (xb + level_shift * g0)
    o_sr = split(combine(xr, orbitals_all))
    r1 = [r0[x] - s1 * a1[x] for x in range(8)]
    ar1 = [b0[x] - s1 * la1[x] + level_shift * o_sr[x] for x in range(8)]

    src_g[2, 0:1] = dots([(ar1, r1), (ar1, ar1)])
    start_sum(src_g.at[2, 0:1], slots_g.at[2, :, 0:1], 4, "gy")
    src_z[2, 0:1] = finish_sum(src_g.at[2, 0:1], slots_g.at[2, :, 0:1], 4)
    start_sum(src_z.at[2, 0:1], slots_z.at[2, :, 0:1], 5, "gx")
    total = finish_sum(src_z.at[2, 0:1], slots_z.at[2, :, 0:1], 5) * (1.0 / cells)
    s2 = pick(total, 0) / (pick(total, 1) + epsilon)

    dens = []
    for x in range(8):
        delta = s1 * r0[x] + s2 * r1[x]
        delta_ref[:, x] = delta.reshape(8, 8, 128)
        dens.append(jnp.sum((delta * own[x]).reshape(8, 8, 128), axis=0))
    shift = lax.rem(128 - 32 * me["band"], 128)
    dens = [pltpu.roll(plane, shift, 1) for plane in dens]
    copies_dens = []
    lane8 = iota((8, 128), 1)
    for d in [2, 1, 3, 0]:
        for half in range(2):
            packed = None
            for j in range(4):
                plane = dens[4 * half + j]
                turn = (32 * (j - d)) % 128
                plane = pltpu.roll(plane, turn, 1) if turn else plane
                packed = plane if packed is None else jnp.where(lane8 // 32 == j, plane, packed)
            dens_src[d, half] = packed
        if d:
            copies_dens.append(send(dens_src.at[d], dens_slots.at[d - 1], dens_sems, d - 1, "band", d))
    for x in range(8):
        residual_ref[:, x] = (r1[x] - s2 * ar1[x]).reshape(8, 8, 128)
    for copy in copies_dens:
        copy.wait_recv()
    for half in range(2):
        total = dens_src[0, half] + dens_slots[0, half] + dens_slots[1, half] + dens_slots[2, half]
        total = total * (4.0 / (8 * n_band))
        for j in range(4):
            plane = pltpu.roll(total, 128 - 32 * j, 1) if j else total
            density_ref[4 * half + j] = plane[:, 0:32]

    for copy in (
        copies_quarter + copies_o + copies_halo + copies_dv + copies_y + copies_ho + copies_gram + copies_b + copies_dens
    ):
        copy.wait_send()
    drain(slots_g.at[0], 0)
    drain(slots_z.at[0], 1)
    drain(slots_g.at[1, :, 0:3], 2)
    drain(slots_z.at[1, :, 0:3], 3)
    drain(slots_g.at[2, :, 0:1], 4)
    drain(slots_z.at[2, :, 0:1], 5)


def shards(sizes, orbitals, delta_potential, potential, energies, band_index):
    n_gx, n_gy, n_band = sizes
    f32 = jnp.float32
    field = (8, 8, 8, 128)
    vmem = pl.BlockSpec(memory_space=pltpu.VMEM)
    hbm = pl.BlockSpec(memory_space=pltpu.HBM)

    def v(*shape):
        return pltpu.VMEM(shape, f32)

    def dma(*shape):
        return pltpu.SemaphoreType.DMA(shape)

    outs = (
        jax.ShapeDtypeStruct(field, f32),
        jax.ShapeDtypeStruct(field, f32),
        jax.ShapeDtypeStruct((8, 8, 128 // n_band), f32),
    )
    return pl.pallas_call(
        functools.partial(kernel, sizes),
        out_shape=outs,
        in_specs=[hbm] * 5,
        out_specs=(vmem, vmem, vmem),
        scratch_shapes=[
            v(4, *field),
            v(4, *field),
            v(8, 8, 128),
            v(8, 8, 128),
            pltpu.SMEM(energies.shape, f32),
            pltpu.SMEM(band_index.shape, jnp.int32),
            v(2, 8, WIDTH, 8, 128),
            v(2, *field),
            v(2, WIDTH, 8, 128),
            v(2, 8, 8, 128),
            v(*field),
            v(2, 8, WIDTH, 8, 128),
            v(2, *field),
            v(8, 64, 128),
            v(4, 4, 128),
            v(3, 4, 128),
            v(3, 4, 128),
            v(3, 4, 128),
            v(3, n_gy - 1, 4, 128),
            v(3, n_gx - 1, 4, 128),
            v(4, 2, 128),
            v(4, 2, 8, 128),
            v(3, 2, 8, 128),
            dma(5),
            pltpu.SemaphoreType.REGULAR((3,)),
            dma(2, 15),
            dma(2, 6),
            dma(2, 12),
            dma(2, 6),
            dma(2, 6),
            dma(2, 3),
        ],
        compiler_params=pltpu.CompilerParams(
            collective_id=0, has_side_effects=True, vmem_limit_bytes=48 * 2**20
        ),
        name="sternheimer",
    )(
        *[
            pltpu.with_memory_space_constraint(a, pltpu.HBM)
            for a in (orbitals, delta_potential, potential, energies, band_index)
        ]
    )

def solution(mesh):
    sizes = tuple(mesh.shape[a] for a in ("gx", "gy", "band"))
    return jax.shard_map(
        functools.partial(shards, sizes),
        mesh=mesh,
        in_specs=(
            P("band", "gx", "gy", None),
            P("gx", "gy", None),
            P("gx", "gy", None),
            P(),
            P("band"),
        ),
        out_specs=(P("band", "gx", "gy", None), P("band", "gx", "gy", None), P("gx", "gy", "band")),
        check_vma=False,
    )
```

```python
import functools

import jax
import jax.numpy as jnp
from jax import lax
from jax.experimental import pallas as pl
from jax.experimental.pallas import tpu as pltpu
from jax.sharding import PartitionSpec as P

stencil_weights = (
    -5369.0 / 1800.0,
    12.0 / 7.0,
    -15.0 / 56.0,
    10.0 / 189.0,
    -1.0 / 112.0,
    2.0 / 1925.0,
    -1.0 / 16632.0,
)
spacing = 0.6
level_shift = 4.0
epsilon = 1e-06
highest = lax.Precision.HIGHEST
scale = -0.5 / (spacing * spacing)
taps = tuple(scale * w for w in stencil_weights)
MESH = pl.DeviceIdType.MESH
WIDTH = 6


def iota(shape, dim):
    return lax.broadcasted_iota(jnp.int32, shape, dim)


def dot(a, b):
    return jnp.dot(a, b, precision=highest, preferred_element_type=jnp.float32)


def dot_nt(a, b):
    return lax.dot_general(
        a, b, (((1,), (1,)), ((), ())), precision=highest, preferred_element_type=jnp.float32
    )


def thirds(x):
    high = x.astype(jnp.bfloat16)
    rest = x - high.astype(jnp.float32)
    middle = rest.astype(jnp.bfloat16)
    low = (rest - middle.astype(jnp.float32)).astype(jnp.bfloat16)
    return [high, middle, low]


def dot_parts(a, parts, dims=(1, 0)):
    pieces = thirds(a)
    size = a.shape[0]
    orders = [None, None, None]
    for i, part in enumerate(parts):
        product = lax.dot_general(
            jnp.concatenate(pieces[: 3 - i], axis=0),
            part,
            (((dims[0],), (dims[1],)), ((), ())),
            preferred_element_type=jnp.float32,
        )
        for j in range(3 - i):
            term = product[size * j : size * j + size]
            orders[i + j] = term if orders[i + j] is None else orders[i + j] + term
    return orders[0] + (orders[1] + orders[2])


def rowsum(x):
    return jnp.sum(x, axis=1, keepdims=True)


def lanes(parts):
    return jnp.concatenate(parts, axis=1)


def rows(parts):
    return jnp.concatenate(parts, axis=0)


def kernel(
    sizes,
    o_hbm,
    dv_hbm,
    v_hbm,
    energies_hbm,
    index_hbm,
    delta_ref,
    residual_ref,
    density_ref,
    o_all,
    ho_all,
    dv_ref,
    v_ref,
    energies_ref,
    index_ref,
    x_halo,
    y_halo,
    dvx_halo,
    dvy_halo,
    b_own,
    bx_halo,
    by_halo,
    hp_keep,
    src_y,
    slots_y,
    src_g,
    src_z,
    slots_g,
    slots_z,
    near_slots,
    far_slots,
    gram_all,
    dens_src,
    dens_slots,
    load_sems,
    relay_sems,
    quarter_sems,
    gather_sems,
    halo_sems,
    sum_sems,
    gram_sems,
    dens_sems,
):
    n_gx, n_gy, n_band = sizes
    me = {a: lax.axis_index(a) for a in ("gx", "gy", "band")}
    count = {"gx": n_gx, "gy": n_gy, "band": n_band}
    cells = float(n_gx * n_gy * 8 * 8 * 128)
    mine = me["band"]

    def peer(axis, offset):
        return {axis: lax.rem(me[axis] + offset, count[axis])}

    loads = [
        pltpu.make_async_copy(src, dst, load_sems.at[i])
        for i, (src, dst) in enumerate(
            [
                (o_hbm, o_all.at[mine]),
                (dv_hbm, dv_ref),
                (v_hbm, v_ref),
                (energies_hbm, energies_ref),
                (index_hbm, index_ref),
            ]
        )
    ]
    for copy in loads:
        copy.start()
    barrier = pltpu.get_barrier_semaphore()
    partners = 0
    sides = (1, n_gx - 1)
    for axis, offsets in (("gx", sides), ("gy", range(1, n_gy)), ("band", range(1, n_band))):
        for offset in offsets:
            pl.semaphore_signal(barrier, inc=1, device_id=peer(axis, offset), device_id_type=MESH)
            partners += 1
    for copy in loads:
        copy.wait()
    pl.semaphore_wait(barrier, partners)

    def send(src, dst, sems, k, axis, offset):
        copy = pltpu.make_async_remote_copy(
            src_ref=src,
            dst_ref=dst,
            send_sem=sems.at[0, k],
            recv_sem=sems.at[1, k],
            device_id=peer(axis, offset),
            device_id_type=MESH,
        )
        copy.start()
        return copy

    def tell(step):
        for offset in (2**step, n_gx - 2**step):
            pl.semaphore_signal(
                relay_sems.at[step], inc=1, device_id=peer("gx", offset), device_id_type=MESH
            )

    def hear(step):
        pl.semaphore_wait(relay_sems.at[step], 2)

    far = [2, 1, 3]

    def part(x):
        return o_all.at[mine, :, pl.ds(2 * x, 2)]

    copies_quarter = []
    for d in far:
        x = lax.rem(mine + d, 4)
        copies_quarter.append(send(part(x), part(x), quarter_sems, d - 1, "band", d))

    def halo_gx(field, xh, base):
        return [
            send(field.at[:, 8 - WIDTH : 8], xh.at[0], halo_sems, base, "gx", 1),
            send(field.at[:, 0:WIDTH], xh.at[1], halo_sems, base + 1, "gx", n_gx - 1),
        ]

    def halo_gy(field, yh, base):
        return [
            send(field, yh.at[0], halo_sems, base + 2, "gy", 1),
            send(field, yh.at[1], halo_sems, base + 3, "gy", n_gy - 1),
        ]

    copies_halo = halo_gx(o_all.at[mine], x_halo, 0) + halo_gy(o_all.at[mine], y_halo, 0)
    copies_dv = [
        send(dv_ref.at[8 - WIDTH : 8], dvx_halo.at[0], halo_sems, 8, "gx", 1),
        send(dv_ref.at[0:WIDTH], dvx_halo.at[1], halo_sems, 9, "gx", n_gx - 1),
        send(dv_ref, dvy_halo.at[0], halo_sems, 10, "gy", 1),
        send(dv_ref, dvy_halo.at[1], halo_sems, 11, "gy", n_gy - 1),
    ]
    left, right = lax.rem(mine + 3, 4), lax.rem(mine + 1, 4)
    opposite = lax.rem(mine + 2, 4)

    def rows_of(ref, band, start, size):
        return ref.at[band, :, pl.ds(start, size)]

    def pass_on(ref, band, pieces, sems, base, d):
        out = []
        for i, (start, size) in enumerate(pieces):
            piece = rows_of(ref, band, start, size)
            out.append(send(piece, piece, sems, base + i, "band", d))
        return out

    to_right = pass_on(o_all, mine, [(2 * left, 2)], quarter_sems, 3, 1)
    to_left = pass_on(o_all, mine, [(2 * right, 2)], quarter_sems, 7, 3)

    tell(0)

    low_x = jnp.where(me["gx"] > 0, 1.0, 0.0).astype(jnp.float32)
    high_x = jnp.where(me["gx"] < n_gx - 1, 1.0, 0.0).astype(jnp.float32)
    low_y = jnp.where(me["gy"] > 0, 1.0, 0.0).astype(jnp.float32)
    high_y = jnp.where(me["gy"] < n_gy - 1, 1.0, 0.0).astype(jnp.float32)

    def weights_of(distance, center):
        out = jnp.where(distance == 0, center, 0.0)
        for k in range(1, 7):
            out = jnp.where(distance == k, taps[k], out)
        return out.astype(jnp.float32)

    za, zb = iota((128, 128), 0), iota((128, 128), 1)
    zd = jnp.abs(za - zb)
    along_z = weights_of(jnp.minimum(zd, 128 - zd), 3.0 * taps[0])
    ra, rb = iota((64, 64), 0), iota((64, 64), 1)
    same = ra // 8 == rb // 8
    ya, yb = ra % 8, rb % 8
    along_y = lanes(
        [
            jnp.where(same, weights_of(ya - (yb - 8), 0.0), 0.0) * low_y,
            jnp.where(same, weights_of(jnp.abs(ya - yb), 0.0), 0.0),
            jnp.where(same, weights_of(yb + 8 - ya, 0.0), 0.0) * high_y,
        ]
    )
    diag = jnp.where(iota((64, 256), 0) % 8 == iota((64, 256), 1) % 8, 1.0, 0.0).astype(jnp.float32)
    fold = jnp.where(iota((256, 128), 0) // 8 == iota((256, 128), 1) % 32, 1.0, 0.0).astype(
        jnp.bfloat16
    )
    unfold = jnp.where(iota((128, 256), 0) % 32 == iota((128, 256), 1) // 8, 1.0, 0.0).astype(
        jnp.bfloat16
    )
    ones = jnp.ones((128, 128), jnp.bfloat16)
    row_n = iota((64, 128), 0) // 8
    lane = iota((64, 128), 1)
    group = jnp.where(lane // 32 == row_n % 4, 1.0, 0.0).astype(jnp.float32)

    levels = rows(
        [jnp.full((8, 128), energies_ref[index_ref[n]], jnp.float32) for n in range(8)]
    )

    def slab(ref, x):
        return ref[:, x].reshape(64, 128)

    def slabs(ref):
        return [slab(ref, x) for x in range(8)]

    def over_bands(plane):
        return rows([plane] * 8)

    def hamiltonian(cur, x_low, x_high, y_low, y_high):
        ny = dot(along_y, rows([lanes(y_low), lanes(cur), lanes(y_high)]))
        nz = dot(rows(cur), along_z)
        line = [x_low[i] * low_x for i in range(6)] + cur + [x_high[i] * high_x for i in range(6)]
        out = []
        for x in range(8):
            total = over_bands(v_ref[x]) * cur[x]
            for k in range(1, 7):
                total = total + taps[k] * (line[x + 6 + k] + line[x + 6 - k])
            out.append(total + ny[:, 128 * x : 128 * x + 128] + nz[64 * x : 64 * x + 64])
        return out

    def column(ref, x):
        return rows([ref[q, :, x].reshape(64, 128) for q in range(4)])

    def stacked(ref):
        return lanes([column(ref, x) for x in range(8)])

    def packed(t):
        t = t * group
        return rows(
            [jnp.sum(t[0:32], axis=0, keepdims=True), jnp.sum(t[32:64], axis=0, keepdims=True)]
        )

    def intersect(field, everything):
        return packed(dot_parts(dot_parts(lanes(field), everything, (1, 1)) * diag, [fold]))

    def dots(pairs):
        parts = []
        for a, b in pairs:
            total = a[0] * b[0]
            for x in range(1, 8):
                total = total + a[x] * b[x]
            parts.append(total)
        stack = rows(parts)
        shape = stack.shape
        total = dot_parts(stack, [ones])
        total = jnp.where(iota(shape, 0) // 8 == iota(shape, 1), total, 0.0)
        return jnp.sum(total, axis=0, keepdims=True)

    def pick(row, q):
        return rowsum(jnp.where(lane == row_n + 8 * q, row, 0.0))

    def expand(packed):
        full = rows(
            [jnp.broadcast_to(packed[0:1], (32, 128)), jnp.broadcast_to(packed[1:2], (32, 128))]
        )
        return full * group

    def spread(x_form):
        return dot_parts(x_form, [unfold]) * diag

    def combine(x_form, everything):
        return dot_parts(spread(x_form), everything)

    def split(wide):
        return [wide[:, 128 * x : 128 * x + 128] for x in range(8)]

    near = [4, 12, 3, 13, 2, 14, 1, 15]

    def far_copy(dz, dy):
        return pltpu.make_async_remote_copy(
            src_ref=src_g.at[2, 0:1],
            dst_ref=far_slots.at[(dz - 5) * n_gy + dy],
            send_sem=sum_sems.at[0, 6],
            recv_sem=sum_sems.at[1, 6],
            device_id={
                "gx": lax.rem(me["gx"] + dz, n_gx),
                "gy": lax.rem(me["gy"] + dy, n_gy),
            },
            device_id_type=MESH,
        )

    def start_sum(src, slots, k, axis, some=None):
        n = count[axis]
        sems = sum_sems
        order = sorted(range(1, n), key=lambda d: -min(d, n - d))
        for i, d in enumerate(some or order):
            pltpu.make_async_remote_copy(
                src_ref=src,
                dst_ref=slots.at[i if some else d - 1],
                send_sem=sems.at[0, k],
                recv_sem=sems.at[1, k],
                device_id=peer(axis, d),
                device_id_type=MESH,
            ).start()

    def finish_sum(src, slots, k):
        pltpu.make_async_copy(slots, slots, sum_sems.at[1, k]).wait()
        total = src[...]
        for d in range(slots.shape[0]):
            total = total + slots[d]
        return total

    def drain(slots, k):
        pltpu.make_async_copy(slots, slots, sum_sems.at[0, k]).wait()

    hear(0)
    tell(1)
    for copy in copies_quarter:
        copy.wait_recv()
    pieces, pieces_p = [], []
    for i in range(2):
        piece = column(o_all, 2 * mine + i)
        pieces.append(piece)
        pieces_p.append(piece * rows([dv_ref[2 * mine + i]] * 32))
    quarter = lanes(pieces)
    t = dot_nt(rows([lanes(pieces_p), quarter]), quarter) * rows([diag] * 8)
    t = dot_parts(t, [fold])
    for q in range(4):
        src_y[q, 0:2] = packed(t[64 * q : 64 * q + 64])
        src_y[q, 2:4] = packed(t[256 + 64 * q : 256 + 64 * q + 64])
    copies_y = [
        send(src_y.at[lax.rem(mine + d, 4)], slots_y.at[d - 1], gram_sems, d - 1, "band", d)
        for d in far
    ]

    low, high = (2 * mine, 1), (2 * mine + 1, 1)
    to_right += pass_on(o_all, mine, [low, high, (2 * opposite, 2)], quarter_sems, 4, 1)
    to_left += pass_on(o_all, mine, [high, low, (2 * opposite, 2)], quarter_sems, 8, 3)

    for copy in copies_halo:
        copy.wait_recv()
    own = slabs(o_all.at[mine])
    ox_low, ox_high = ([slab(x_halo.at[side], i) for i in range(WIDTH)] for side in (0, 1))
    oy_low, oy_high = (slabs(y_halo.at[side]) for side in (0, 1))
    ho = hamiltonian(own, ox_low, ox_high, oy_low, oy_high)
    for x in range(8):
        ho_all[mine, :, x] = ho[x].reshape(8, 8, 128)
    ho_right = pass_on(ho_all, mine, [(0, 4), (4, 4)], gather_sems, 0, 1)
    ho_left = pass_on(ho_all, mine, [(4, 4), (0, 4)], gather_sems, 2, 3)

    hear(1)
    tell(2)
    for copy in copies_y:
        copy.wait_recv()
    src_g[0] = src_y[mine] + slots_y[0] + slots_y[1] + slots_y[2]
    start_sum(src_g.at[0], slots_g.at[0], 0, "gy")

    for copy in to_right[:2] + to_left[:2]:
        copy.wait_recv()
    onward = pass_on(o_all, left, [(2 * opposite, 2), (2 * left, 1)], quarter_sems, 11, 1)
    onward += pass_on(o_all, right, [(2 * opposite, 2), (2 * right + 1, 1)], quarter_sems, 13, 3)
    copies_o = to_right + to_left + onward

    for copy in copies_dv:
        copy.wait_recv()
    perturbed = [own[x] * over_bands(dv_ref[x]) for x in range(8)]
    hp = hamiltonian(
        perturbed,
        [ox_low[i] * over_bands(dvx_halo[0, i]) for i in range(WIDTH)],
        [ox_high[i] * over_bands(dvx_halo[1, i]) for i in range(WIDTH)],
        [oy_low[x] * over_bands(dvy_halo[0, x]) for x in range(8)],
        [oy_high[x] * over_bands(dvy_halo[1, x]) for x in range(8)],
    )
    for x in range(8):
        hp_keep[x] = hp[x]

    hear(2)
    src_z[0] = finish_sum(src_g.at[0], slots_g.at[0], 0)
    start_sum(src_z.at[0], slots_z.at[0], 1, "gx")

    for copy in [ho_right[0], ho_left[0]]:
        copy.wait_recv()
    copies_ho = ho_right + ho_left
    copies_ho += pass_on(ho_all, left, [(0, 4)], gather_sems, 4, 1)
    copies_ho += pass_on(ho_all, right, [(4, 4)], gather_sems, 5, 3)
    for copy in to_right[2:] + to_left[2:] + onward:
        copy.wait_recv()
    orbitals_all = thirds(stacked(o_all))
    total = finish_sum(src_z.at[0], slots_z.at[0], 1) * (1.0 / cells)
    gram_all[mine] = total[2:4]
    copies_gram = [
        send(gram_all.at[mine], gram_all.at[mine], gram_sems, 2 + d, "band", d) for d in far
    ]
    for copy in ho_right[1:] + ho_left[1:] + copies_ho[4:]:
        copy.wait_recv()
    h_orbitals_all = thirds(stacked(ho_all))
    x1 = expand(total[0:2])
    w1 = spread(x1)
    o_s1, ho_s1 = split(dot_parts(w1, orbitals_all)), split(dot_parts(w1, h_orbitals_all))
    r0 = [o_s1[x] - perturbed[x] for x in range(8)]
    b0 = [ho_s1[x] - hp_keep[x] - levels * r0[x] for x in range(8)]
    for x in range(8):
        b_own[:, x] = b0[x].reshape(8, 8, 128)
    copies_b = halo_gx(b_own, bx_halo, 4)

    src_g[1, 0:2] = intersect(b0, orbitals_all)
    src_g[1, 2:3] = dots([(b0, r0), (b0, b0)])
    start_sum(src_g.at[1, 0:3], slots_g.at[1, :, 0:3], 2, "gy")
    copies_b += halo_gy(b_own, by_halo, 4)

    src_z[1, 0:3] = finish_sum(src_g.at[1, 0:3], slots_g.at[1, :, 0:3], 2)
    start_sum(src_z.at[1, 0:3], slots_z.at[1, :, 0:3], 3, "gx")

    for copy in copies_gram:
        copy.wait_recv()
    gram = rows([jnp.broadcast_to(gram_all[q, r : r + 1], (8, 128)) for q in range(4) for r in range(2)])
    pick_rows = jnp.where(
        iota((32, 64), 1) == 8 * (iota((32, 64), 0) // 4), 1.0, 0.0
    ).astype(jnp.float32)
    gram = jnp.where(iota((32, 128), 1) // 32 == iota((32, 128), 0) % 4, dot(pick_rows, gram), 0.0)
    repeat = jnp.where(iota((128, 128), 0) % 32 == iota((128, 128), 1) % 32, 1.0, 0.0).astype(
        jnp.float32
    )
    gram = dot(gram, repeat)
    gram_blocks = jnp.where(
        iota((128, 128), 0) // 32 == iota((128, 128), 1) // 32, rows([gram] * 4), 0.0
    )
    x0 = dot(x1, gram_blocks) - x1
    g0 = dot(x0, gram_blocks)
    w0 = spread(x0)
    o_s0, ho_s0 = split(dot_parts(w0, orbitals_all)), split(dot_parts(w0, h_orbitals_all))

    for copy in copies_b:
        copy.wait_recv()
    lb = hamiltonian(
        b0,
        [slab(bx_halo.at[0], i) for i in range(WIDTH)],
        [slab(bx_halo.at[1], i) for i in range(WIDTH)],
        slabs(by_halo.at[0]),
        slabs(by_halo.at[1]),
    )
    a1 = [b0[x] + level_shift * o_s0[x] for x in range(8)]
    la1 = [
        lb[x] - levels * b0[x] + level_shift * (ho_s0[x] - levels * o_s0[x]) for x in range(8)
    ]

    total = finish_sum(src_z.at[1, 0:3], slots_z.at[1, :, 0:3], 3) * (1.0 / cells)
    xb = expand(total[0:2])
    dots_row = total[2:3]
    numerator = pick(dots_row, 0) + level_shift * rowsum(x0 * x0)
    denominator = pick(dots_row, 1) + rowsum(
        2.0 * level_shift * x0 * xb + (level_shift * level_shift) * x0 * g0
    )
    s1 = numerator / (denominator + epsilon)
    xr = x0 - s1 * (xb + level_shift * g0)
    o_sr = split(combine(xr, orbitals_all))
    r1 = [r0[x] - s1 * a1[x] for x in range(8)]
    ar1 = [b0[x] - s1 * la1[x] + level_shift * o_sr[x] for x in range(8)]

    src_g[2, 0:1] = dots([(ar1, r1), (ar1, ar1)])
    start_sum(src_g.at[2, 0:1], slots_g.at[2, :, 0:1], 4, "gy")

    def send_far(i, carry):
        dz = 8 + ((i + 1) // 2) * (1 - 2 * (i % 2))
        for dy in range(n_gy):
            far_copy(dz, dy).start()
        return carry

    lax.fori_loop(0, 7, send_far, 0)
    src_z[2, 0:1] = finish_sum(src_g.at[2, 0:1], slots_g.at[2, :, 0:1], 4)
    start_sum(src_z.at[2, 0:1], near_slots, 5, "gx", near)
    parts = [src_z[2, 0:1], jnp.zeros((1, 128), jnp.float32)]
    pltpu.make_async_copy(near_slots, near_slots, sum_sems.at[1, 5]).wait()
    for i in range(len(near)):
        parts[i % 2] = parts[i % 2] + near_slots[i]
    pltpu.make_async_copy(far_slots, far_slots, sum_sems.at[1, 6]).wait()
    for i in range(7 * n_gy):
        parts[i % 2] = parts[i % 2] + far_slots[i]
    total = (parts[0] + parts[1]) * (1.0 / cells)
    s2 = pick(total, 0) / (pick(total, 1) + epsilon)

    dens = []
    for x in range(8):
        delta = s1 * r0[x] + s2 * r1[x]
        delta_ref[:, x] = delta.reshape(8, 8, 128)
        dens.append(jnp.sum((delta * own[x]).reshape(8, 8, 128), axis=0))
    shift = lax.rem(128 - 32 * me["band"], 128)
    dens = [pltpu.roll(plane, shift, 1) for plane in dens]
    copies_dens = []
    lane8 = iota((8, 128), 1)
    for d in [2, 1, 3, 0]:
        for half in range(2):
            packed = None
            for j in range(4):
                plane = dens[4 * half + j]
                turn = (32 * (j - d)) % 128
                plane = pltpu.roll(plane, turn, 1) if turn else plane
                packed = plane if packed is None else jnp.where(lane8 // 32 == j, plane, packed)
            dens_src[d, half] = packed
        if d:
            copies_dens.append(send(dens_src.at[d], dens_slots.at[d - 1], dens_sems, d - 1, "band", d))
    for x in range(8):
        residual_ref[:, x] = (r1[x] - s2 * ar1[x]).reshape(8, 8, 128)
    for copy in copies_dens:
        copy.wait_recv()
    for half in range(2):
        total = dens_src[0, half] + dens_slots[0, half] + dens_slots[1, half] + dens_slots[2, half]
        total = total * (4.0 / (8 * n_band))
        for j in range(4):
            plane = pltpu.roll(total, 128 - 32 * j, 1) if j else total
            density_ref[4 * half + j] = plane[:, 0:32]

    for copy in (
        copies_quarter + copies_o + copies_halo + copies_dv + copies_y + copies_ho + copies_gram + copies_b + copies_dens
    ):
        copy.wait_send()
    drain(slots_g.at[0], 0)
    drain(slots_z.at[0], 1)
    drain(slots_g.at[1, :, 0:3], 2)
    drain(slots_z.at[1, :, 0:3], 3)
    drain(slots_g.at[2, :, 0:1], 4)
    drain(near_slots, 5)
    drain(far_slots, 6)


def shards(sizes, orbitals, delta_potential, potential, energies, band_index):
    n_gx, n_gy, n_band = sizes
    f32 = jnp.float32
    field = (8, 8, 8, 128)
    vmem = pl.BlockSpec(memory_space=pltpu.VMEM)
    hbm = pl.BlockSpec(memory_space=pltpu.HBM)

    def v(*shape):
        return pltpu.VMEM(shape, f32)

    def dma(*shape):
        return pltpu.SemaphoreType.DMA(shape)

    outs = (
        jax.ShapeDtypeStruct(field, f32),
        jax.ShapeDtypeStruct(field, f32),
        jax.ShapeDtypeStruct((8, 8, 128 // n_band), f32),
    )
    return pl.pallas_call(
        functools.partial(kernel, sizes),
        out_shape=outs,
        in_specs=[hbm] * 5,
        out_specs=(vmem, vmem, vmem),
        scratch_shapes=[
            v(4, *field),
            v(4, *field),
            v(8, 8, 128),
            v(8, 8, 128),
            pltpu.SMEM(energies.shape, f32),
            pltpu.SMEM(band_index.shape, jnp.int32),
            v(2, 8, WIDTH, 8, 128),
            v(2, *field),
            v(2, WIDTH, 8, 128),
            v(2, 8, 8, 128),
            v(*field),
            v(2, 8, WIDTH, 8, 128),
            v(2, *field),
            v(8, 64, 128),
            v(4, 4, 128),
            v(3, 4, 128),
            v(3, 4, 128),
            v(3, 4, 128),
            v(3, n_gy - 1, 4, 128),
            v(3, n_gx - 1, 4, 128),
            v(8, 1, 128),
            v(7 * n_gy, 1, 128),
            v(4, 2, 128),
            v(4, 2, 8, 128),
            v(3, 2, 8, 128),
            dma(5),
            pltpu.SemaphoreType.REGULAR((3,)),
            dma(2, 15),
            dma(2, 6),
            dma(2, 12),
            dma(2, 7),
            dma(2, 6),
            dma(2, 3),
        ],
        compiler_params=pltpu.CompilerParams(
            collective_id=0, has_side_effects=True, vmem_limit_bytes=48 * 2**20
        ),
        name="sternheimer",
    )(
        *[
            pltpu.with_memory_space_constraint(a, pltpu.HBM)
            for a in (orbitals, delta_potential, potential, energies, band_index)
        ]
    )

def solution(mesh):
    sizes = tuple(mesh.shape[a] for a in ("gx", "gy", "band"))
    return jax.shard_map(
        functools.partial(shards, sizes),
        mesh=mesh,
        in_specs=(
            P("band", "gx", "gy", None),
            P("gx", "gy", None),
            P("gx", "gy", None),
            P(),
            P("band"),
        ),
        out_specs=(P("band", "gx", "gy", None), P("band", "gx", "gy", None), P("gx", "gy", "band")),
        check_vma=False,
    )
```

```python
import functools

import jax
import jax.numpy as jnp
from jax import lax
from jax.experimental import pallas as pl
from jax.experimental.pallas import tpu as pltpu
from jax.sharding import PartitionSpec as P

stencil_weights = (
    -5369.0 / 1800.0,
    12.0 / 7.0,
    -15.0 / 56.0,
    10.0 / 189.0,
    -1.0 / 112.0,
    2.0 / 1925.0,
    -1.0 / 16632.0,
)
spacing = 0.6
level_shift = 4.0
epsilon = 1e-06
highest = lax.Precision.HIGHEST
scale = -0.5 / (spacing * spacing)
taps = tuple(scale * w for w in stencil_weights)
MESH = pl.DeviceIdType.MESH
WIDTH = 6


def iota(shape, dim):
    return lax.broadcasted_iota(jnp.int32, shape, dim)


def dot(a, b):
    return jnp.dot(a, b, precision=highest, preferred_element_type=jnp.float32)


def dot_nt(a, b):
    return lax.dot_general(
        a, b, (((1,), (1,)), ((), ())), precision=highest, preferred_element_type=jnp.float32
    )


def thirds(x):
    high = x.astype(jnp.bfloat16)
    rest = x - high.astype(jnp.float32)
    middle = rest.astype(jnp.bfloat16)
    low = (rest - middle.astype(jnp.float32)).astype(jnp.bfloat16)
    return [high, middle, low]


def dot_parts(a, parts, dims=(1, 0)):
    pieces = thirds(a)
    size = a.shape[0]
    orders = [None, None, None]
    for i, part in enumerate(parts):
        product = lax.dot_general(
            jnp.concatenate(pieces[: 3 - i], axis=0),
            part,
            (((dims[0],), (dims[1],)), ((), ())),
            preferred_element_type=jnp.float32,
        )
        for j in range(3 - i):
            term = product[size * j : size * j + size]
            orders[i + j] = term if orders[i + j] is None else orders[i + j] + term
    return orders[0] + (orders[1] + orders[2])


def rowsum(x):
    return jnp.sum(x, axis=1, keepdims=True)


def lanes(parts):
    return jnp.concatenate(parts, axis=1)


def rows(parts):
    return jnp.concatenate(parts, axis=0)


def kernel(
    sizes,
    o_hbm,
    dv_hbm,
    v_hbm,
    energies_hbm,
    index_hbm,
    delta_ref,
    residual_ref,
    density_ref,
    o_all,
    ho_all,
    dv_ref,
    v_ref,
    energies_ref,
    index_ref,
    x_halo,
    y_halo,
    dvx_halo,
    dvy_halo,
    b_own,
    bx_halo,
    by_halo,
    hp_keep,
    src_y,
    slots_y,
    src_g,
    src_z,
    slots_g,
    slots_z,
    near_slots,
    far_slots,
    gram_all,
    dens_src,
    dens_slots,
    load_sems,
    relay_sems,
    quarter_sems,
    gather_sems,
    halo_sems,
    sum_sems,
    gram_sems,
    dens_sems,
):
    n_gx, n_gy, n_band = sizes
    me = {a: lax.axis_index(a) for a in ("gx", "gy", "band")}
    count = {"gx": n_gx, "gy": n_gy, "band": n_band}
    cells = float(n_gx * n_gy * 8 * 8 * 128)
    mine = me["band"]

    def peer(axis, offset):
        return {axis: lax.rem(me[axis] + offset, count[axis])}

    loads = [
        pltpu.make_async_copy(src, dst, load_sems.at[i])
        for i, (src, dst) in enumerate(
            [
                (o_hbm, o_all.at[mine]),
                (dv_hbm, dv_ref),
                (v_hbm, v_ref),
                (energies_hbm, energies_ref),
                (index_hbm, index_ref),
            ]
        )
    ]
    for copy in loads:
        copy.start()
    barrier = pltpu.get_barrier_semaphore()
    partners = 0
    sides = (1, n_gx - 1)
    for axis, offsets in (("gx", sides), ("gy", range(1, n_gy)), ("band", range(1, n_band))):
        for offset in offsets:
            pl.semaphore_signal(barrier, inc=1, device_id=peer(axis, offset), device_id_type=MESH)
            partners += 1
    for copy in loads:
        copy.wait()
    pl.semaphore_wait(barrier, partners)

    def send(src, dst, sems, k, axis, offset):
        copy = pltpu.make_async_remote_copy(
            src_ref=src,
            dst_ref=dst,
            send_sem=sems.at[0, k],
            recv_sem=sems.at[1, k],
            device_id=peer(axis, offset),
            device_id_type=MESH,
        )
        copy.start()
        return copy

    def tell(step):
        for offset in (2**step, n_gx - 2**step):
            pl.semaphore_signal(
                relay_sems.at[step], inc=1, device_id=peer("gx", offset), device_id_type=MESH
            )

    def hear(step):
        pl.semaphore_wait(relay_sems.at[step], 2)

    far = [2, 1, 3]

    def part(x):
        return o_all.at[mine, :, pl.ds(2 * x, 2)]

    copies_quarter = []
    for d in far:
        x = lax.rem(mine + d, 4)
        copies_quarter.append(send(part(x), part(x), quarter_sems, d - 1, "band", d))

    def halo_gx(field, xh, base):
        return [
            send(field.at[:, 8 - WIDTH : 8], xh.at[0], halo_sems, base, "gx", 1),
            send(field.at[:, 0:WIDTH], xh.at[1], halo_sems, base + 1, "gx", n_gx - 1),
        ]

    def halo_gy(field, yh, base):
        return [
            send(field, yh.at[0], halo_sems, base + 2, "gy", 1),
            send(field, yh.at[1], halo_sems, base + 3, "gy", n_gy - 1),
        ]

    copies_halo = halo_gx(o_all.at[mine], x_halo, 0) + halo_gy(o_all.at[mine], y_halo, 0)
    copies_dv = [
        send(dv_ref.at[8 - WIDTH : 8], dvx_halo.at[0], halo_sems, 8, "gx", 1),
        send(dv_ref.at[0:WIDTH], dvx_halo.at[1], halo_sems, 9, "gx", n_gx - 1),
        send(dv_ref, dvy_halo.at[0], halo_sems, 10, "gy", 1),
        send(dv_ref, dvy_halo.at[1], halo_sems, 11, "gy", n_gy - 1),
    ]
    left, right = lax.rem(mine + 3, 4), lax.rem(mine + 1, 4)
    opposite = lax.rem(mine + 2, 4)

    def rows_of(ref, band, start, size):
        return ref.at[band, :, pl.ds(start, size)]

    def pass_on(ref, band, pieces, sems, base, d):
        out = []
        for i, (start, size) in enumerate(pieces):
            piece = rows_of(ref, band, start, size)
            out.append(send(piece, piece, sems, base + i, "band", d))
        return out

    low, high = (2 * mine, 1), (2 * mine + 1, 1)
    to_right = pass_on(o_all, mine, [(2 * left, 2), low], quarter_sems, 3, 1)
    to_left = pass_on(o_all, mine, [(2 * right, 2), high], quarter_sems, 7, 3)

    tell(0)

    low_x = jnp.where(me["gx"] > 0, 1.0, 0.0).astype(jnp.float32)
    high_x = jnp.where(me["gx"] < n_gx - 1, 1.0, 0.0).astype(jnp.float32)
    low_y = jnp.where(me["gy"] > 0, 1.0, 0.0).astype(jnp.float32)
    high_y = jnp.where(me["gy"] < n_gy - 1, 1.0, 0.0).astype(jnp.float32)

    def weights_of(distance, center):
        out = jnp.where(distance == 0, center, 0.0)
        for k in range(1, 7):
            out = jnp.where(distance == k, taps[k], out)
        return out.astype(jnp.float32)

    za, zb = iota((128, 128), 0), iota((128, 128), 1)
    zd = jnp.abs(za - zb)
    along_z = weights_of(jnp.minimum(zd, 128 - zd), 3.0 * taps[0])
    ra, rb = iota((64, 64), 0), iota((64, 64), 1)
    same = ra // 8 == rb // 8
    ya, yb = ra % 8, rb % 8
    along_y = lanes(
        [
            jnp.where(same, weights_of(ya - (yb - 8), 0.0), 0.0) * low_y,
            jnp.where(same, weights_of(jnp.abs(ya - yb), 0.0), 0.0),
            jnp.where(same, weights_of(yb + 8 - ya, 0.0), 0.0) * high_y,
        ]
    )
    diag = jnp.where(iota((64, 256), 0) % 8 == iota((64, 256), 1) % 8, 1.0, 0.0).astype(jnp.float32)
    fold = jnp.where(iota((256, 128), 0) // 8 == iota((256, 128), 1) % 32, 1.0, 0.0).astype(
        jnp.bfloat16
    )
    unfold = jnp.where(iota((128, 256), 0) % 32 == iota((128, 256), 1) // 8, 1.0, 0.0).astype(
        jnp.bfloat16
    )
    ones = jnp.ones((128, 128), jnp.bfloat16)
    row_n = iota((64, 128), 0) // 8
    lane = iota((64, 128), 1)
    group = jnp.where(lane // 32 == row_n % 4, 1.0, 0.0).astype(jnp.float32)

    levels = rows(
        [jnp.full((8, 128), energies_ref[index_ref[n]], jnp.float32) for n in range(8)]
    )

    def slab(ref, x):
        return ref[:, x].reshape(64, 128)

    def slabs(ref):
        return [slab(ref, x) for x in range(8)]

    def over_bands(plane):
        return rows([plane] * 8)

    def hamiltonian(cur, x_low, x_high, y_low, y_high):
        ny = dot(along_y, rows([lanes(y_low), lanes(cur), lanes(y_high)]))
        nz = dot(rows(cur), along_z)
        line = [x_low[i] * low_x for i in range(6)] + cur + [x_high[i] * high_x for i in range(6)]
        out = []
        for x in range(8):
            total = over_bands(v_ref[x]) * cur[x]
            for k in range(1, 7):
                total = total + taps[k] * (line[x + 6 + k] + line[x + 6 - k])
            out.append(total + ny[:, 128 * x : 128 * x + 128] + nz[64 * x : 64 * x + 64])
        return out

    def column(ref, x):
        return rows([ref[q, :, x].reshape(64, 128) for q in range(4)])

    def stacked(ref):
        return lanes([column(ref, x) for x in range(8)])

    def packed(t):
        t = t * group
        return rows(
            [jnp.sum(t[0:32], axis=0, keepdims=True), jnp.sum(t[32:64], axis=0, keepdims=True)]
        )

    def intersect(field, everything):
        return packed(dot_parts(dot_parts(lanes(field), everything, (1, 1)) * diag, [fold]))

    def dots(pairs):
        parts = []
        for a, b in pairs:
            total = a[0] * b[0]
            for x in range(1, 8):
                total = total + a[x] * b[x]
            parts.append(total)
        stack = rows(parts)
        shape = stack.shape
        total = dot_parts(stack, [ones])
        total = jnp.where(iota(shape, 0) // 8 == iota(shape, 1), total, 0.0)
        return jnp.sum(total, axis=0, keepdims=True)

    def pick(row, q):
        return rowsum(jnp.where(lane == row_n + 8 * q, row, 0.0))

    def expand(packed):
        full = rows(
            [jnp.broadcast_to(packed[0:1], (32, 128)), jnp.broadcast_to(packed[1:2], (32, 128))]
        )
        return full * group

    def spread(x_form):
        return dot_parts(x_form, [unfold]) * diag

    def combine(x_form, everything):
        return dot_parts(spread(x_form), everything)

    def split(wide):
        return [wide[:, 128 * x : 128 * x + 128] for x in range(8)]

    near = [4, 12, 3, 13, 2, 14, 1, 15]

    def far_copy(dz, dy):
        return pltpu.make_async_remote_copy(
            src_ref=src_g.at[2, 0:1],
            dst_ref=far_slots.at[(dz - 5) * n_gy + dy],
            send_sem=sum_sems.at[0, 6],
            recv_sem=sum_sems.at[1, 6],
            device_id={
                "gx": lax.rem(me["gx"] + dz, n_gx),
                "gy": lax.rem(me["gy"] + dy, n_gy),
            },
            device_id_type=MESH,
        )

    def start_sum(src, slots, k, axis, some=None):
        n = count[axis]
        sems = sum_sems
        order = sorted(range(1, n), key=lambda d: -min(d, n - d))
        for i, d in enumerate(some or order):
            pltpu.make_async_remote_copy(
                src_ref=src,
                dst_ref=slots.at[i if some else d - 1],
                send_sem=sems.at[0, k],
                recv_sem=sems.at[1, k],
                device_id=peer(axis, d),
                device_id_type=MESH,
            ).start()

    def finish_sum(src, slots, k):
        pltpu.make_async_copy(slots, slots, sum_sems.at[1, k]).wait()
        total = src[...]
        for d in range(slots.shape[0]):
            total = total + slots[d]
        return total

    def drain(slots, k):
        pltpu.make_async_copy(slots, slots, sum_sems.at[0, k]).wait()

    hear(0)
    tell(1)
    for copy in copies_quarter:
        copy.wait_recv()
    pieces, pieces_p = [], []
    for i in range(2):
        piece = column(o_all, 2 * mine + i)
        pieces.append(piece)
        pieces_p.append(piece * rows([dv_ref[2 * mine + i]] * 32))
    quarter = lanes(pieces)
    t = dot_parts(rows([lanes(pieces_p), quarter]), thirds(quarter), (1, 1)) * rows([diag] * 8)
    t = dot_parts(t, [fold])
    for q in range(4):
        src_y[q, 0:2] = packed(t[64 * q : 64 * q + 64])
        src_y[q, 2:4] = packed(t[256 + 64 * q : 256 + 64 * q + 64])
    copies_y = [
        send(src_y.at[lax.rem(mine + d, 4)], slots_y.at[d - 1], gram_sems, d - 1, "band", d)
        for d in far
    ]

    to_right += pass_on(o_all, mine, [high, (2 * opposite, 2)], quarter_sems, 5, 1)
    to_left += pass_on(o_all, mine, [low, (2 * opposite, 2)], quarter_sems, 9, 3)
    for copy in to_right[:2] + to_left[:2]:
        copy.wait_recv()
    onward = pass_on(o_all, left, [(2 * opposite, 2), (2 * left, 1)], quarter_sems, 11, 1)
    onward += pass_on(o_all, right, [(2 * opposite, 2), (2 * right + 1, 1)], quarter_sems, 13, 3)
    copies_o = to_right + to_left + onward

    for copy in copies_halo:
        copy.wait_recv()
    own = slabs(o_all.at[mine])
    ox_low, ox_high = ([slab(x_halo.at[side], i) for i in range(WIDTH)] for side in (0, 1))
    oy_low, oy_high = (slabs(y_halo.at[side]) for side in (0, 1))
    ho = hamiltonian(own, ox_low, ox_high, oy_low, oy_high)
    for x in range(8):
        ho_all[mine, :, x] = ho[x].reshape(8, 8, 128)
    ho_right = pass_on(ho_all, mine, [(0, 4), (4, 4)], gather_sems, 0, 1)
    ho_left = pass_on(ho_all, mine, [(4, 4), (0, 4)], gather_sems, 2, 3)

    hear(1)
    tell(2)
    for copy in copies_y:
        copy.wait_recv()
    src_g[0] = src_y[mine] + slots_y[0] + slots_y[1] + slots_y[2]
    start_sum(src_g.at[0], slots_g.at[0], 0, "gy")


    for copy in copies_dv:
        copy.wait_recv()
    perturbed = [own[x] * over_bands(dv_ref[x]) for x in range(8)]
    hp = hamiltonian(
        perturbed,
        [ox_low[i] * over_bands(dvx_halo[0, i]) for i in range(WIDTH)],
        [ox_high[i] * over_bands(dvx_halo[1, i]) for i in range(WIDTH)],
        [oy_low[x] * over_bands(dvy_halo[0, x]) for x in range(8)],
        [oy_high[x] * over_bands(dvy_halo[1, x]) for x in range(8)],
    )
    for x in range(8):
        hp_keep[x] = hp[x]

    hear(2)
    src_z[0] = finish_sum(src_g.at[0], slots_g.at[0], 0)
    start_sum(src_z.at[0], slots_z.at[0], 1, "gx")

    for copy in [ho_right[0], ho_left[0]]:
        copy.wait_recv()
    copies_ho = ho_right + ho_left
    copies_ho += pass_on(ho_all, left, [(0, 4)], gather_sems, 4, 1)
    copies_ho += pass_on(ho_all, right, [(4, 4)], gather_sems, 5, 3)
    for copy in to_right[2:] + to_left[2:] + onward:
        copy.wait_recv()
    orbitals_all = thirds(stacked(o_all))
    total = finish_sum(src_z.at[0], slots_z.at[0], 1) * (1.0 / cells)
    gram_all[mine] = total[2:4]
    copies_gram = [
        send(gram_all.at[mine], gram_all.at[mine], gram_sems, 2 + d, "band", d) for d in far
    ]
    for copy in ho_right[1:] + ho_left[1:] + copies_ho[4:]:
        copy.wait_recv()
    h_orbitals_all = thirds(stacked(ho_all))
    x1 = expand(total[0:2])
    w1 = spread(x1)
    o_s1, ho_s1 = split(dot_parts(w1, orbitals_all)), split(dot_parts(w1, h_orbitals_all))
    r0 = [o_s1[x] - perturbed[x] for x in range(8)]
    b0 = [ho_s1[x] - hp_keep[x] - levels * r0[x] for x in range(8)]
    for x in range(8):
        b_own[:, x] = b0[x].reshape(8, 8, 128)
    copies_b = halo_gx(b_own, bx_halo, 4)

    src_g[1, 0:2] = intersect(b0, orbitals_all)
    src_g[1, 2:3] = dots([(b0, r0), (b0, b0)])
    start_sum(src_g.at[1, 0:3], slots_g.at[1, :, 0:3], 2, "gy")
    copies_b += halo_gy(b_own, by_halo, 4)

    src_z[1, 0:3] = finish_sum(src_g.at[1, 0:3], slots_g.at[1, :, 0:3], 2)
    start_sum(src_z.at[1, 0:3], slots_z.at[1, :, 0:3], 3, "gx")

    for copy in copies_gram:
        copy.wait_recv()
    gram = rows([jnp.broadcast_to(gram_all[q, r : r + 1], (8, 128)) for q in range(4) for r in range(2)])
    pick_rows = jnp.where(
        iota((32, 64), 1) == 8 * (iota((32, 64), 0) // 4), 1.0, 0.0
    ).astype(jnp.float32)
    gram = jnp.where(iota((32, 128), 1) // 32 == iota((32, 128), 0) % 4, dot(pick_rows, gram), 0.0)
    repeat = jnp.where(iota((128, 128), 0) % 32 == iota((128, 128), 1) % 32, 1.0, 0.0).astype(
        jnp.float32
    )
    gram = dot(gram, repeat)
    gram_blocks = jnp.where(
        iota((128, 128), 0) // 32 == iota((128, 128), 1) // 32, rows([gram] * 4), 0.0
    )
    x0 = dot(x1, gram_blocks) - x1
    g0 = dot(x0, gram_blocks)
    w0 = spread(x0)
    o_s0, ho_s0 = split(dot_parts(w0, orbitals_all)), split(dot_parts(w0, h_orbitals_all))

    for copy in copies_b:
        copy.wait_recv()
    lb = hamiltonian(
        b0,
        [slab(bx_halo.at[0], i) for i in range(WIDTH)],
        [slab(bx_halo.at[1], i) for i in range(WIDTH)],
        slabs(by_halo.at[0]),
        slabs(by_halo.at[1]),
    )
    a1 = [b0[x] + level_shift * o_s0[x] for x in range(8)]
    la1 = [
        lb[x] - levels * b0[x] + level_shift * (ho_s0[x] - levels * o_s0[x]) for x in range(8)
    ]

    total = finish_sum(src_z.at[1, 0:3], slots_z.at[1, :, 0:3], 3) * (1.0 / cells)
    xb = expand(total[0:2])
    dots_row = total[2:3]
    numerator = pick(dots_row, 0) + level_shift * rowsum(x0 * x0)
    denominator = pick(dots_row, 1) + rowsum(
        2.0 * level_shift * x0 * xb + (level_shift * level_shift) * x0 * g0
    )
    s1 = numerator / (denominator + epsilon)
    xr = x0 - s1 * (xb + level_shift * g0)
    o_sr = split(combine(xr, orbitals_all))
    r1 = [r0[x] - s1 * a1[x] for x in range(8)]
    ar1 = [b0[x] - s1 * la1[x] + level_shift * o_sr[x] for x in range(8)]

    src_g[2, 0:1] = dots([(ar1, r1), (ar1, ar1)])
    start_sum(src_g.at[2, 0:1], slots_g.at[2, :, 0:1], 4, "gy")

    def send_far(i, carry):
        dz = 8 + ((i + 1) // 2) * (1 - 2 * (i % 2))
        for dy in range(n_gy):
            far_copy(dz, dy).start()
        return carry

    lax.fori_loop(0, 7, send_far, 0)
    src_z[2, 0:1] = finish_sum(src_g.at[2, 0:1], slots_g.at[2, :, 0:1], 4)
    start_sum(src_z.at[2, 0:1], near_slots, 5, "gx", near)
    parts = [src_z[2, 0:1], jnp.zeros((1, 128), jnp.float32)]
    pltpu.make_async_copy(near_slots, near_slots, sum_sems.at[1, 5]).wait()
    for i in range(len(near)):
        parts[i % 2] = parts[i % 2] + near_slots[i]
    pltpu.make_async_copy(far_slots, far_slots, sum_sems.at[1, 6]).wait()
    for i in range(7 * n_gy):
        parts[i % 2] = parts[i % 2] + far_slots[i]
    total = (parts[0] + parts[1]) * (1.0 / cells)
    s2 = pick(total, 0) / (pick(total, 1) + epsilon)

    dens = []
    for x in range(8):
        delta = s1 * r0[x] + s2 * r1[x]
        delta_ref[:, x] = delta.reshape(8, 8, 128)
        dens.append(jnp.sum((delta * own[x]).reshape(8, 8, 128), axis=0))
    shift = lax.rem(128 - 32 * me["band"], 128)
    dens = [pltpu.roll(plane, shift, 1) for plane in dens]
    copies_dens = []
    lane8 = iota((8, 128), 1)
    for d in [2, 1, 3, 0]:
        for half in range(2):
            packed = None
            for j in range(4):
                plane = dens[4 * half + j]
                turn = (32 * (j - d)) % 128
                plane = pltpu.roll(plane, turn, 1) if turn else plane
                packed = plane if packed is None else jnp.where(lane8 // 32 == j, plane, packed)
            dens_src[d, half] = packed
        if d:
            copies_dens.append(send(dens_src.at[d], dens_slots.at[d - 1], dens_sems, d - 1, "band", d))
    for x in range(8):
        residual_ref[:, x] = (r1[x] - s2 * ar1[x]).reshape(8, 8, 128)
    for copy in copies_dens:
        copy.wait_recv()
    for half in range(2):
        total = dens_src[0, half] + dens_slots[0, half] + dens_slots[1, half] + dens_slots[2, half]
        total = total * (4.0 / (8 * n_band))
        for j in range(4):
            plane = pltpu.roll(total, 128 - 32 * j, 1) if j else total
            density_ref[4 * half + j] = plane[:, 0:32]

    for copy in (
        copies_quarter + copies_o + copies_halo + copies_dv + copies_y + copies_ho + copies_gram + copies_b + copies_dens
    ):
        copy.wait_send()
    drain(slots_g.at[0], 0)
    drain(slots_z.at[0], 1)
    drain(slots_g.at[1, :, 0:3], 2)
    drain(slots_z.at[1, :, 0:3], 3)
    drain(slots_g.at[2, :, 0:1], 4)
    drain(near_slots, 5)
    drain(far_slots, 6)


def shards(sizes, orbitals, delta_potential, potential, energies, band_index):
    n_gx, n_gy, n_band = sizes
    f32 = jnp.float32
    field = (8, 8, 8, 128)
    vmem = pl.BlockSpec(memory_space=pltpu.VMEM)
    hbm = pl.BlockSpec(memory_space=pltpu.HBM)

    def v(*shape):
        return pltpu.VMEM(shape, f32)

    def dma(*shape):
        return pltpu.SemaphoreType.DMA(shape)

    outs = (
        jax.ShapeDtypeStruct(field, f32),
        jax.ShapeDtypeStruct(field, f32),
        jax.ShapeDtypeStruct((8, 8, 128 // n_band), f32),
    )
    return pl.pallas_call(
        functools.partial(kernel, sizes),
        out_shape=outs,
        in_specs=[hbm] * 5,
        out_specs=(vmem, vmem, vmem),
        scratch_shapes=[
            v(4, *field),
            v(4, *field),
            v(8, 8, 128),
            v(8, 8, 128),
            pltpu.SMEM(energies.shape, f32),
            pltpu.SMEM(band_index.shape, jnp.int32),
            v(2, 8, WIDTH, 8, 128),
            v(2, *field),
            v(2, WIDTH, 8, 128),
            v(2, 8, 8, 128),
            v(*field),
            v(2, 8, WIDTH, 8, 128),
            v(2, *field),
            v(8, 64, 128),
            v(4, 4, 128),
            v(3, 4, 128),
            v(3, 4, 128),
            v(3, 4, 128),
            v(3, n_gy - 1, 4, 128),
            v(3, n_gx - 1, 4, 128),
            v(8, 1, 128),
            v(7 * n_gy, 1, 128),
            v(4, 2, 128),
            v(4, 2, 8, 128),
            v(3, 2, 8, 128),
            dma(5),
            pltpu.SemaphoreType.REGULAR((3,)),
            dma(2, 15),
            dma(2, 6),
            dma(2, 12),
            dma(2, 7),
            dma(2, 6),
            dma(2, 3),
        ],
        compiler_params=pltpu.CompilerParams(
            collective_id=0, has_side_effects=True, vmem_limit_bytes=48 * 2**20
        ),
        name="sternheimer",
    )(
        *[
            pltpu.with_memory_space_constraint(a, pltpu.HBM)
            for a in (orbitals, delta_potential, potential, energies, band_index)
        ]
    )

def solution(mesh):
    sizes = tuple(mesh.shape[a] for a in ("gx", "gy", "band"))
    return jax.shard_map(
        functools.partial(shards, sizes),
        mesh=mesh,
        in_specs=(
            P("band", "gx", "gy", None),
            P("gx", "gy", None),
            P("gx", "gy", None),
            P(),
            P("band"),
        ),
        out_specs=(P("band", "gx", "gy", None), P("band", "gx", "gy", None), P("gx", "gy", "band")),
        check_vma=False,
    )
```

```python
import functools

import jax
import jax.numpy as jnp
from jax import lax
from jax.experimental import pallas as pl
from jax.experimental.pallas import tpu as pltpu
from jax.sharding import PartitionSpec as P

stencil_weights = (
    -5369.0 / 1800.0,
    12.0 / 7.0,
    -15.0 / 56.0,
    10.0 / 189.0,
    -1.0 / 112.0,
    2.0 / 1925.0,
    -1.0 / 16632.0,
)
spacing = 0.6
level_shift = 4.0
epsilon = 1e-06
highest = lax.Precision.HIGHEST
scale = -0.5 / (spacing * spacing)
taps = tuple(scale * w for w in stencil_weights)
MESH = pl.DeviceIdType.MESH
WIDTH = 6


def iota(shape, dim):
    return lax.broadcasted_iota(jnp.int32, shape, dim)


def dot(a, b):
    return jnp.dot(a, b, precision=highest, preferred_element_type=jnp.float32)


def dot_nt(a, b):
    return lax.dot_general(
        a, b, (((1,), (1,)), ((), ())), precision=highest, preferred_element_type=jnp.float32
    )


def thirds(x):
    high = x.astype(jnp.bfloat16)
    rest = x - high.astype(jnp.float32)
    middle = rest.astype(jnp.bfloat16)
    low = (rest - middle.astype(jnp.float32)).astype(jnp.bfloat16)
    return [high, middle, low]


def dot_parts(a, parts, dims=(1, 0)):
    pieces = thirds(a)
    size = a.shape[0]
    orders = [None, None, None]
    for i, part in enumerate(parts):
        product = lax.dot_general(
            jnp.concatenate(pieces[: 3 - i], axis=0),
            part,
            (((dims[0],), (dims[1],)), ((), ())),
            preferred_element_type=jnp.float32,
        )
        for j in range(3 - i):
            term = product[size * j : size * j + size]
            orders[i + j] = term if orders[i + j] is None else orders[i + j] + term
    return orders[0] + (orders[1] + orders[2])


def rowsum(x):
    return jnp.sum(x, axis=1, keepdims=True)


def lanes(parts):
    return jnp.concatenate(parts, axis=1)


def rows(parts):
    return jnp.concatenate(parts, axis=0)


def kernel(
    sizes,
    o_hbm,
    dv_hbm,
    v_hbm,
    energies_hbm,
    index_hbm,
    r0_ref,
    r1_ref,
    ar1_ref,
    steps_ref,
    density_ref,
    o_all,
    ho_all,
    dv_ref,
    v_ref,
    energies_ref,
    index_ref,
    x_halo,
    y_halo,
    dvx_halo,
    dvy_halo,
    b_own,
    bx_halo,
    by_halo,
    hp_keep,
    src_y,
    slots_y,
    src_g,
    src_z,
    slots_g,
    slots_z,
    near_slots,
    far_slots,
    gram_all,
    dens_src,
    dens_slots,
    load_sems,
    relay_sems,
    quarter_sems,
    gather_sems,
    halo_sems,
    sum_sems,
    gram_sems,
    dens_sems,
):
    n_gx, n_gy, n_band = sizes
    me = {a: lax.axis_index(a) for a in ("gx", "gy", "band")}
    count = {"gx": n_gx, "gy": n_gy, "band": n_band}
    cells = float(n_gx * n_gy * 8 * 8 * 128)
    mine = me["band"]

    def peer(axis, offset):
        return {axis: lax.rem(me[axis] + offset, count[axis])}

    loads = [
        pltpu.make_async_copy(src, dst, load_sems.at[i])
        for i, (src, dst) in enumerate(
            [
                (o_hbm, o_all.at[mine]),
                (dv_hbm, dv_ref),
                (v_hbm, v_ref),
                (energies_hbm, energies_ref),
                (index_hbm, index_ref),
            ]
        )
    ]
    for copy in loads:
        copy.start()
    barrier = pltpu.get_barrier_semaphore()
    partners = 0
    sides = (1, n_gx - 1)
    for axis, offsets in (("gx", sides), ("gy", range(1, n_gy)), ("band", range(1, n_band))):
        for offset in offsets:
            pl.semaphore_signal(barrier, inc=1, device_id=peer(axis, offset), device_id_type=MESH)
            partners += 1
    for copy in loads:
        copy.wait()
    pl.semaphore_wait(barrier, partners)

    def send(src, dst, sems, k, axis, offset):
        copy = pltpu.make_async_remote_copy(
            src_ref=src,
            dst_ref=dst,
            send_sem=sems.at[0, k],
            recv_sem=sems.at[1, k],
            device_id=peer(axis, offset),
            device_id_type=MESH,
        )
        copy.start()
        return copy

    def tell(step):
        for offset in (2**step, n_gx - 2**step):
            pl.semaphore_signal(
                relay_sems.at[step], inc=1, device_id=peer("gx", offset), device_id_type=MESH
            )

    def hear(step):
        pl.semaphore_wait(relay_sems.at[step], 2)

    far = [2, 1, 3]

    def part(x):
        return o_all.at[mine, :, pl.ds(2 * x, 2)]

    copies_quarter = []
    for d in far:
        x = lax.rem(mine + d, 4)
        copies_quarter.append(send(part(x), part(x), quarter_sems, d - 1, "band", d))

    def halo_gx(field, xh, base):
        return [
            send(field.at[:, 8 - WIDTH : 8], xh.at[0], halo_sems, base, "gx", 1),
            send(field.at[:, 0:WIDTH], xh.at[1], halo_sems, base + 1, "gx", n_gx - 1),
        ]

    def halo_gy(field, yh, base):
        return [
            send(field, yh.at[0], halo_sems, base + 2, "gy", 1),
            send(field, yh.at[1], halo_sems, base + 3, "gy", n_gy - 1),
        ]

    copies_halo = halo_gx(o_all.at[mine], x_halo, 0) + halo_gy(o_all.at[mine], y_halo, 0)
    copies_dv = [
        send(dv_ref.at[8 - WIDTH : 8], dvx_halo.at[0], halo_sems, 8, "gx", 1),
        send(dv_ref.at[0:WIDTH], dvx_halo.at[1], halo_sems, 9, "gx", n_gx - 1),
        send(dv_ref, dvy_halo.at[0], halo_sems, 10, "gy", 1),
        send(dv_ref, dvy_halo.at[1], halo_sems, 11, "gy", n_gy - 1),
    ]
    left, right = lax.rem(mine + 3, 4), lax.rem(mine + 1, 4)
    opposite = lax.rem(mine + 2, 4)

    def rows_of(ref, band, start, size):
        return ref.at[band, :, pl.ds(start, size)]

    def pass_on(ref, band, pieces, sems, base, d):
        out = []
        for i, (start, size) in enumerate(pieces):
            piece = rows_of(ref, band, start, size)
            out.append(send(piece, piece, sems, base + i, "band", d))
        return out

    low, high = (2 * mine, 1), (2 * mine + 1, 1)
    to_right = pass_on(o_all, mine, [(2 * left, 2), low], quarter_sems, 3, 1)
    to_left = pass_on(o_all, mine, [(2 * right, 2), high], quarter_sems, 7, 3)

    tell(0)

    low_x = jnp.where(me["gx"] > 0, 1.0, 0.0).astype(jnp.float32)
    high_x = jnp.where(me["gx"] < n_gx - 1, 1.0, 0.0).astype(jnp.float32)
    low_y = jnp.where(me["gy"] > 0, 1.0, 0.0).astype(jnp.float32)
    high_y = jnp.where(me["gy"] < n_gy - 1, 1.0, 0.0).astype(jnp.float32)

    def weights_of(distance, center):
        out = jnp.where(distance == 0, center, 0.0)
        for k in range(1, 7):
            out = jnp.where(distance == k, taps[k], out)
        return out.astype(jnp.float32)

    za, zb = iota((128, 128), 0), iota((128, 128), 1)
    zd = jnp.abs(za - zb)
    along_z = weights_of(jnp.minimum(zd, 128 - zd), 3.0 * taps[0])
    along_z = thirds(along_z)
    ra, rb = iota((64, 64), 0), iota((64, 64), 1)
    same = ra // 8 == rb // 8
    ya, yb = ra % 8, rb % 8
    along_y = lanes(
        [
            jnp.where(same, weights_of(ya - (yb - 8), 0.0), 0.0) * low_y,
            jnp.where(same, weights_of(jnp.abs(ya - yb), 0.0), 0.0),
            jnp.where(same, weights_of(yb + 8 - ya, 0.0), 0.0) * high_y,
        ]
    )
    diag = jnp.where(iota((64, 256), 0) % 8 == iota((64, 256), 1) % 8, 1.0, 0.0).astype(jnp.float32)
    fold = jnp.where(iota((256, 128), 0) // 8 == iota((256, 128), 1) % 32, 1.0, 0.0).astype(
        jnp.bfloat16
    )
    unfold = jnp.where(iota((128, 256), 0) % 32 == iota((128, 256), 1) // 8, 1.0, 0.0).astype(
        jnp.bfloat16
    )
    ones = jnp.ones((128, 128), jnp.bfloat16)
    row_n = iota((64, 128), 0) // 8
    lane = iota((64, 128), 1)
    group = jnp.where(lane // 32 == row_n % 4, 1.0, 0.0).astype(jnp.float32)

    levels = rows(
        [jnp.full((8, 128), energies_ref[index_ref[n]], jnp.float32) for n in range(8)]
    )

    def slab(ref, x):
        return ref[:, x].reshape(64, 128)

    def slabs(ref):
        return [slab(ref, x) for x in range(8)]

    def over_bands(plane):
        return rows([plane] * 8)

    def hamiltonian(cur, x_low, x_high, y_low, y_high):
        ny = dot_parts(along_y, thirds(rows([lanes(y_low), lanes(cur), lanes(y_high)])))
        nz = dot_parts(rows(cur), along_z)
        line = [x_low[i] * low_x for i in range(6)] + cur + [x_high[i] * high_x for i in range(6)]
        out = []
        for x in range(8):
            total = over_bands(v_ref[x]) * cur[x]
            for k in range(1, 7):
                total = total + taps[k] * (line[x + 6 + k] + line[x + 6 - k])
            out.append(total + ny[:, 128 * x : 128 * x + 128] + nz[64 * x : 64 * x + 64])
        return out

    def column(ref, x):
        return rows([ref[q, :, x].reshape(64, 128) for q in range(4)])

    def stacked(ref):
        return lanes([column(ref, x) for x in range(8)])

    def packed(t):
        t = t * group
        return rows(
            [jnp.sum(t[0:32], axis=0, keepdims=True), jnp.sum(t[32:64], axis=0, keepdims=True)]
        )

    def intersect(field, everything):
        return packed(dot_parts(dot_parts(lanes(field), everything, (1, 1)) * diag, [fold]))

    def dots(pairs):
        parts = []
        for a, b in pairs:
            total = a[0] * b[0]
            for x in range(1, 8):
                total = total + a[x] * b[x]
            parts.append(total)
        stack = rows(parts)
        shape = stack.shape
        total = jnp.broadcast_to(rowsum(stack), shape)
        total = jnp.where(iota(shape, 0) // 8 == iota(shape, 1), total, 0.0)
        return jnp.sum(total, axis=0, keepdims=True)

    def pick(row, q):
        return rowsum(jnp.where(lane == row_n + 8 * q, row, 0.0))

    def expand(packed):
        full = rows(
            [jnp.broadcast_to(packed[0:1], (32, 128)), jnp.broadcast_to(packed[1:2], (32, 128))]
        )
        return full * group

    def spread(x_form):
        return dot_parts(x_form, [unfold]) * diag

    def combine(x_form, everything):
        return dot_parts(spread(x_form), everything)

    def split(wide):
        return [wide[:, 128 * x : 128 * x + 128] for x in range(8)]

    near = [4, 12, 3, 13, 2, 14, 1, 15]

    def far_copy(dz, dy):
        return pltpu.make_async_remote_copy(
            src_ref=src_g.at[2, 0:1],
            dst_ref=far_slots.at[(dz - 5) * n_gy + dy],
            send_sem=sum_sems.at[0, 6],
            recv_sem=sum_sems.at[1, 6],
            device_id={
                "gx": lax.rem(me["gx"] + dz, n_gx),
                "gy": lax.rem(me["gy"] + dy, n_gy),
            },
            device_id_type=MESH,
        )

    def start_sum(src, slots, k, axis, some=None):
        n = count[axis]
        sems = sum_sems
        order = sorted(range(1, n), key=lambda d: -min(d, n - d))
        for i, d in enumerate(some or order):
            pltpu.make_async_remote_copy(
                src_ref=src,
                dst_ref=slots.at[i if some else d - 1],
                send_sem=sems.at[0, k],
                recv_sem=sems.at[1, k],
                device_id=peer(axis, d),
                device_id_type=MESH,
            ).start()

    def finish_sum(src, slots, k):
        pltpu.make_async_copy(slots, slots, sum_sems.at[1, k]).wait()
        total = src[...]
        for d in range(slots.shape[0]):
            total = total + slots[d]
        return total

    def drain(slots, k):
        pltpu.make_async_copy(slots, slots, sum_sems.at[0, k]).wait()

    hear(0)
    tell(1)
    for copy in copies_quarter:
        copy.wait_recv()
    pieces, pieces_p = [], []
    for i in range(2):
        piece = column(o_all, 2 * mine + i)
        pieces.append(piece)
        pieces_p.append(piece * rows([dv_ref[2 * mine + i]] * 32))
    quarter = lanes(pieces)
    t = dot_parts(rows([lanes(pieces_p), quarter]), thirds(quarter), (1, 1)) * rows([diag] * 8)
    t = dot_parts(t, [fold])
    for q in range(4):
        src_y[q, 0:2] = packed(t[64 * q : 64 * q + 64])
        src_y[q, 2:4] = packed(t[256 + 64 * q : 256 + 64 * q + 64])
    copies_y = [
        send(src_y.at[lax.rem(mine + d, 4)], slots_y.at[d - 1], gram_sems, d - 1, "band", d)
        for d in far
    ]

    to_right += pass_on(o_all, mine, [high, (2 * opposite, 2)], quarter_sems, 5, 1)
    to_left += pass_on(o_all, mine, [low, (2 * opposite, 2)], quarter_sems, 9, 3)
    for copy in to_right[:2] + to_left[:2]:
        copy.wait_recv()
    onward = pass_on(o_all, left, [(2 * opposite, 2), (2 * left, 1)], quarter_sems, 11, 1)
    onward += pass_on(o_all, right, [(2 * opposite, 2), (2 * right + 1, 1)], quarter_sems, 13, 3)
    copies_o = to_right + to_left + onward

    for copy in copies_halo:
        copy.wait_recv()
    own = slabs(o_all.at[mine])
    ox_low, ox_high = ([slab(x_halo.at[side], i) for i in range(WIDTH)] for side in (0, 1))
    oy_low, oy_high = (slabs(y_halo.at[side]) for side in (0, 1))
    ho = hamiltonian(own, ox_low, ox_high, oy_low, oy_high)
    for x in range(8):
        ho_all[mine, :, x] = ho[x].reshape(8, 8, 128)
    ho_right = pass_on(ho_all, mine, [(0, 4), (4, 4)], gather_sems, 0, 1)
    ho_left = pass_on(ho_all, mine, [(4, 4), (0, 4)], gather_sems, 2, 3)

    hear(1)
    tell(2)
    for copy in copies_y:
        copy.wait_recv()
    src_g[0] = src_y[mine] + slots_y[0] + slots_y[1] + slots_y[2]
    start_sum(src_g.at[0], slots_g.at[0], 0, "gy")


    for copy in copies_dv:
        copy.wait_recv()
    perturbed = [own[x] * over_bands(dv_ref[x]) for x in range(8)]
    hp = hamiltonian(
        perturbed,
        [ox_low[i] * over_bands(dvx_halo[0, i]) for i in range(WIDTH)],
        [ox_high[i] * over_bands(dvx_halo[1, i]) for i in range(WIDTH)],
        [oy_low[x] * over_bands(dvy_halo[0, x]) for x in range(8)],
        [oy_high[x] * over_bands(dvy_halo[1, x]) for x in range(8)],
    )
    for x in range(8):
        hp_keep[x] = hp[x]

    hear(2)
    src_z[0] = finish_sum(src_g.at[0], slots_g.at[0], 0)
    start_sum(src_z.at[0], slots_z.at[0], 1, "gx")

    for copy in [ho_right[0], ho_left[0]]:
        copy.wait_recv()
    copies_ho = ho_right + ho_left
    copies_ho += pass_on(ho_all, left, [(0, 4)], gather_sems, 4, 1)
    copies_ho += pass_on(ho_all, right, [(4, 4)], gather_sems, 5, 3)
    for copy in to_right[2:] + to_left[2:] + onward:
        copy.wait_recv()
    orbitals_all = thirds(stacked(o_all))
    total = finish_sum(src_z.at[0], slots_z.at[0], 1) * (1.0 / cells)
    gram_all[mine] = total[2:4]
    copies_gram = [
        send(gram_all.at[mine], gram_all.at[mine], gram_sems, 2 + d, "band", d) for d in far
    ]
    for copy in ho_right[1:] + ho_left[1:] + copies_ho[4:]:
        copy.wait_recv()
    h_orbitals_all = thirds(stacked(ho_all))
    x1 = expand(total[0:2])
    w1 = spread(x1)
    o_s1, ho_s1 = split(dot_parts(w1, orbitals_all)), split(dot_parts(w1, h_orbitals_all))
    r0 = [o_s1[x] - perturbed[x] for x in range(8)]
    b0 = [ho_s1[x] - hp_keep[x] - levels * r0[x] for x in range(8)]
    for x in range(8):
        b_own[:, x] = b0[x].reshape(8, 8, 128)
    copies_b = halo_gx(b_own, bx_halo, 4)

    src_g[1, 0:2] = intersect(b0, orbitals_all)
    src_g[1, 2:3] = dots([(b0, r0), (b0, b0)])
    start_sum(src_g.at[1, 0:3], slots_g.at[1, :, 0:3], 2, "gy")
    copies_b += halo_gy(b_own, by_halo, 4)

    src_z[1, 0:3] = finish_sum(src_g.at[1, 0:3], slots_g.at[1, :, 0:3], 2)
    start_sum(src_z.at[1, 0:3], slots_z.at[1, :, 0:3], 3, "gx")

    for copy in copies_gram:
        copy.wait_recv()
    gram = rows([jnp.broadcast_to(gram_all[q, r : r + 1], (8, 128)) for q in range(4) for r in range(2)])
    pick_rows = jnp.where(
        iota((32, 64), 1) == 8 * (iota((32, 64), 0) // 4), 1.0, 0.0
    ).astype(jnp.float32)
    gram = jnp.where(iota((32, 128), 1) // 32 == iota((32, 128), 0) % 4, dot(pick_rows, gram), 0.0)
    repeat = jnp.where(iota((128, 128), 0) % 32 == iota((128, 128), 1) % 32, 1.0, 0.0).astype(
        jnp.float32
    )
    gram = dot(gram, repeat)
    gram_blocks = jnp.where(
        iota((128, 128), 0) // 32 == iota((128, 128), 1) // 32, rows([gram] * 4), 0.0
    )
    x0 = dot(x1, gram_blocks) - x1
    g0 = dot(x0, gram_blocks)
    w0 = spread(x0)
    o_s0, ho_s0 = split(dot_parts(w0, orbitals_all)), split(dot_parts(w0, h_orbitals_all))

    for copy in copies_b:
        copy.wait_recv()
    lb = hamiltonian(
        b0,
        [slab(bx_halo.at[0], i) for i in range(WIDTH)],
        [slab(bx_halo.at[1], i) for i in range(WIDTH)],
        slabs(by_halo.at[0]),
        slabs(by_halo.at[1]),
    )
    a1 = [b0[x] + level_shift * o_s0[x] for x in range(8)]
    la1 = [
        lb[x] - levels * b0[x] + level_shift * (ho_s0[x] - levels * o_s0[x]) for x in range(8)
    ]

    total = finish_sum(src_z.at[1, 0:3], slots_z.at[1, :, 0:3], 3) * (1.0 / cells)
    xb = expand(total[0:2])
    dots_row = total[2:3]
    numerator = pick(dots_row, 0) + level_shift * rowsum(x0 * x0)
    denominator = pick(dots_row, 1) + rowsum(
        2.0 * level_shift * x0 * xb + (level_shift * level_shift) * x0 * g0
    )
    s1 = numerator / (denominator + epsilon)
    xr = x0 - s1 * (xb + level_shift * g0)
    o_sr = split(combine(xr, orbitals_all))
    r1 = [r0[x] - s1 * a1[x] for x in range(8)]
    ar1 = [b0[x] - s1 * la1[x] + level_shift * o_sr[x] for x in range(8)]

    src_g[2, 0:1] = dots([(ar1, r1), (ar1, ar1)])
    start_sum(src_g.at[2, 0:1], slots_g.at[2, :, 0:1], 4, "gy")

    def send_far(i, carry):
        dz = 8 + ((i + 1) // 2) * (1 - 2 * (i % 2))
        for dy in range(n_gy):
            far_copy(dz, dy).start()
        return carry

    lax.fori_loop(0, 7, send_far, 0)
    src_z[2, 0:1] = finish_sum(src_g.at[2, 0:1], slots_g.at[2, :, 0:1], 4)
    start_sum(src_z.at[2, 0:1], near_slots, 5, "gx", near)
    parts = [src_z[2, 0:1], jnp.zeros((1, 128), jnp.float32)]
    pltpu.make_async_copy(near_slots, near_slots, sum_sems.at[1, 5]).wait()
    for i in range(len(near)):
        parts[i % 2] = parts[i % 2] + near_slots[i]
    pltpu.make_async_copy(far_slots, far_slots, sum_sems.at[1, 6]).wait()
    for i in range(7 * n_gy):
        parts[i % 2] = parts[i % 2] + far_slots[i]
    total = (parts[0] + parts[1]) * (1.0 / cells)
    s2 = pick(total, 0) / (pick(total, 1) + epsilon)

    dens = []
    for x in range(8):
        delta = s1 * r0[x] + s2 * r1[x]
        dens.append(jnp.sum((delta * own[x]).reshape(8, 8, 128), axis=0))
    shift = lax.rem(128 - 32 * me["band"], 128)
    dens = [pltpu.roll(plane, shift, 1) for plane in dens]
    copies_dens = []
    lane8 = iota((8, 128), 1)
    for d in [2, 1, 3, 0]:
        for half in range(2):
            packed = None
            for j in range(4):
                plane = dens[4 * half + j]
                turn = (32 * (j - d)) % 128
                plane = pltpu.roll(plane, turn, 1) if turn else plane
                packed = plane if packed is None else jnp.where(lane8 // 32 == j, plane, packed)
            dens_src[d, half] = packed
        if d:
            copies_dens.append(send(dens_src.at[d], dens_slots.at[d - 1], dens_sems, d - 1, "band", d))
    for x in range(8):
        r0_ref[:, x] = r0[x].reshape(8, 8, 128)
        r1_ref[:, x] = r1[x].reshape(8, 8, 128)
        ar1_ref[:, x] = ar1[x].reshape(8, 8, 128)
    steps_ref[0] = jnp.broadcast_to(s1, (64, 128)).reshape(8, 8, 128)
    steps_ref[1] = jnp.broadcast_to(s2, (64, 128)).reshape(8, 8, 128)
    for copy in copies_dens:
        copy.wait_recv()
    for half in range(2):
        total = dens_src[0, half] + dens_slots[0, half] + dens_slots[1, half] + dens_slots[2, half]
        total = total * (4.0 / (8 * n_band))
        for j in range(4):
            plane = pltpu.roll(total, 128 - 32 * j, 1) if j else total
            density_ref[4 * half + j] = plane[:, 0:32]

    for copy in (
        copies_quarter + copies_o + copies_halo + copies_dv + copies_y + copies_ho + copies_gram + copies_b + copies_dens
    ):
        copy.wait_send()
    drain(slots_g.at[0], 0)
    drain(slots_z.at[0], 1)
    drain(slots_g.at[1, :, 0:3], 2)
    drain(slots_z.at[1, :, 0:3], 3)
    drain(slots_g.at[2, :, 0:1], 4)
    drain(near_slots, 5)
    drain(far_slots, 6)


def shards(sizes, orbitals, delta_potential, potential, energies, band_index):
    n_gx, n_gy, n_band = sizes
    f32 = jnp.float32
    field = (8, 8, 8, 128)
    vmem = pl.BlockSpec(memory_space=pltpu.VMEM)
    hbm = pl.BlockSpec(memory_space=pltpu.HBM)

    def v(*shape):
        return pltpu.VMEM(shape, f32)

    def dma(*shape):
        return pltpu.SemaphoreType.DMA(shape)

    outs = (
        jax.ShapeDtypeStruct(field, f32),
        jax.ShapeDtypeStruct(field, f32),
        jax.ShapeDtypeStruct(field, f32),
        jax.ShapeDtypeStruct((2, 8, 8, 128), f32),
        jax.ShapeDtypeStruct((8, 8, 128 // n_band), f32),
    )
    r0, r1, ar1, steps, density = pl.pallas_call(
        functools.partial(kernel, sizes),
        out_shape=outs,
        in_specs=[hbm] * 5,
        out_specs=(vmem,) * 5,
        scratch_shapes=[
            v(4, *field),
            v(4, *field),
            v(8, 8, 128),
            v(8, 8, 128),
            pltpu.SMEM(energies.shape, f32),
            pltpu.SMEM(band_index.shape, jnp.int32),
            v(2, 8, WIDTH, 8, 128),
            v(2, *field),
            v(2, WIDTH, 8, 128),
            v(2, 8, 8, 128),
            v(*field),
            v(2, 8, WIDTH, 8, 128),
            v(2, *field),
            v(8, 64, 128),
            v(4, 4, 128),
            v(3, 4, 128),
            v(3, 4, 128),
            v(3, 4, 128),
            v(3, n_gy - 1, 4, 128),
            v(3, n_gx - 1, 4, 128),
            v(8, 1, 128),
            v(7 * n_gy, 1, 128),
            v(4, 2, 128),
            v(4, 2, 8, 128),
            v(3, 2, 8, 128),
            dma(5),
            pltpu.SemaphoreType.REGULAR((3,)),
            dma(2, 15),
            dma(2, 6),
            dma(2, 12),
            dma(2, 7),
            dma(2, 6),
            dma(2, 3),
        ],
        compiler_params=pltpu.CompilerParams(
            collective_id=0, has_side_effects=True, vmem_limit_bytes=48 * 2**20
        ),
        name="sternheimer",
    )(
        *[
            pltpu.with_memory_space_constraint(a, pltpu.HBM)
            for a in (orbitals, delta_potential, potential, energies, band_index)
        ]
    )
    s1, s2 = steps[0][:, None], steps[1][:, None]
    return s1 * r0 + s2 * r1, r1 - s2 * ar1, density


def solution(mesh):
    sizes = tuple(mesh.shape[a] for a in ("gx", "gy", "band"))
    return jax.shard_map(
        functools.partial(shards, sizes),
        mesh=mesh,
        in_specs=(
            P("band", "gx", "gy", None),
            P("gx", "gy", None),
            P("gx", "gy", None),
            P(),
            P("band"),
        ),
        out_specs=(P("band", "gx", "gy", None), P("band", "gx", "gy", None), P("gx", "gy", "band")),
        check_vma=False,
    )
```
